256 devices in a mesh: dp: 64 (over x, z, y_lo), head: 4 (over y_hi, core).
Axes of the slice: x: 4, y: 4 (y_hi: 2, y_lo: 2; y = y_hi * 2 + y_lo), z: 8, core: 2. Of those that a mesh axis runs over, the one named last changes fastest.
Arguments:
- feat_img: bfloat16 [8192, 1280], P('dp'), as said below
- feat_txt: bfloat16 [8192, 1280], P('dp'), as said below
- w_img: bfloat16 [1280, 1024], P(None, 'head'), as said below
- w_txt: bfloat16 [1280, 1024], P(None, 'head'), as said below
- logit_scale: float32 [], replicated, may hold values from 10 to 100
Outputs:
- grad_w_img: float32 [1280, 1024], P('dp', 'head')
- grad_w_txt: float32 [1280, 1024], P('dp', 'head')
The draws below stay inside these ranges and needn't reach their ends.
Inputs may be any that keep to these rules, and one draw needn't show every extreme that they name: `feat_img`: Real-valued features; rows differ in scale. `feat_txt`: Real-valued features. `w_img`: entries of order 1280 ** -0.5. `w_txt`: entries of order 1280 ** -0.5.
All inputs are finite; a program needn't handle non-finite values.
Results may differ from the reference program's by a relative error of at most 0.0041.
Values may be sent and summed in bfloat16 or wider, within the bound.
A program may use at most 128 MiB of HBM per device.

```python
import math
import jax
import jax.numpy as jnp
from jax import lax

D_IN = 1280
EMB = 1024
TOTAL = 8192


def base_features(key):
    return jax.random.normal(key, (TOTAL, D_IN), jnp.float32)


def base_weight(key):
    return jax.random.normal(jax.random.fold_in(key, 901), (D_IN, EMB), jnp.float32) / math.sqrt(D_IN)


def draw_feat_img(key, part):
    image = base_features(key)
    key = jax.random.fold_in(key, 11)
    expo = jax.random.uniform(key, (TOTAL, 1), jnp.float32)
    return (image * jnp.exp(expo * math.log(3.0))).astype(jnp.bfloat16)


def draw_feat_txt(key, part):
    image = base_features(key)
    key = jax.random.fold_in(key, 12)
    own = jax.random.normal(key, (TOTAL, D_IN), jnp.float32)
    rowid = jnp.arange(TOTAL)[:, None] % 61
    mixed = jnp.where(rowid == 0, image + 0.3 * own, own)
    return mixed.astype(jnp.bfloat16)


def draw_w_img(key, part):
    return base_weight(key).astype(jnp.bfloat16)


def draw_w_txt(key, part):
    shared = base_weight(key)
    key = jax.random.fold_in(key, 14)
    own = jax.random.normal(key, (D_IN, EMB), jnp.float32) / math.sqrt(D_IN)
    return (0.7 * shared + 0.7 * own).astype(jnp.bfloat16)


def draw_logit_scale(key, part):
    key = jax.random.fold_in(key, 15)
    return jax.random.uniform(key, (), jnp.float32, 10.0, 20.0)


def setup_inputs(seed: int = 0) -> dict:
    key_list = jax.random.split(jax.random.key(seed), 6)
    return {
        "feat_img": draw_feat_img(jax.random.fold_in(key_list[5], 71), 0),
        "feat_txt": draw_feat_txt(jax.random.fold_in(key_list[5], 71), 0),
        "w_img": draw_w_img(jax.random.fold_in(key_list[5], 71), 0),
        "w_txt": draw_w_txt(jax.random.fold_in(key_list[5], 71), 0),
        "logit_scale": draw_logit_scale(jax.random.fold_in(key_list[5], 71), 0),
    }


def embed(features, weight):
    raw = jnp.dot(features, weight, preferred_element_type=jnp.float32)
    inverse = lax.rsqrt(lax.optimization_barrier(jnp.sum(raw * raw, axis=1, keepdims=True)) + 1e-06)
    return (raw * inverse, inverse)

def backproject(unit, inverse, demb):
    inner = lax.optimization_barrier(jnp.sum(unit * demb, axis=1, keepdims=True))
    return (inverse * (demb - unit * inner)).astype(jnp.bfloat16)

def reference(feat_img, feat_txt, w_img, w_txt, logit_scale):
    img_unit, img_inv = embed(feat_img, w_img)
    txt_unit, txt_inv = embed(feat_txt, w_txt)
    img_emb = img_unit.astype(jnp.bfloat16)
    txt_emb = txt_unit.astype(jnp.bfloat16)
    logits = logit_scale * jnp.dot(img_emb, txt_emb.T, preferred_element_type=jnp.float32)
    row_lse = jax.nn.logsumexp(logits, axis=1, keepdims=True)
    col_lse = jax.nn.logsumexp(logits, axis=0, keepdims=True)
    total = logits.shape[0]
    ident = (lax.broadcasted_iota(jnp.int32, logits.shape, 0) == lax.broadcasted_iota(jnp.int32, logits.shape, 1)).astype(jnp.float32)
    factor = 1.0 / (2.0 * jnp.sqrt(jnp.float32(total)))
    grad_logits = ((jnp.exp(logits - row_lse) + jnp.exp(logits - col_lse) - 2.0 * ident) * factor).astype(jnp.bfloat16)
    img_demb = logit_scale * jnp.dot(grad_logits, txt_emb, preferred_element_type=jnp.float32)
    txt_demb = logit_scale * jnp.dot(grad_logits.T, img_emb, preferred_element_type=jnp.float32)
    img_draw = backproject(img_unit, img_inv, img_demb)
    txt_draw = backproject(txt_unit, txt_inv, txt_demb)
    grad_w_img = jnp.dot(feat_img.T, img_draw, preferred_element_type=jnp.float32)
    grad_w_txt = jnp.dot(feat_txt.T, txt_draw, preferred_element_type=jnp.float32)
    return (grad_w_img, grad_w_txt)
```

```python
import functools

import jax
import jax.numpy as jnp
from jax import lax
from jax.experimental import pallas as pl
from jax.experimental.pallas import tpu as pltpu
from jax.sharding import PartitionSpec as P

MESH = pl.DeviceIdType.MESH
F32 = jnp.float32
BF16 = jnp.bfloat16


def device(x, y, z, core):
    return {"dp": (x * 8 + z) * 2 + y % 2, "head": (y // 2) * 2 + core}


def place():
    d = lax.axis_index("dp")
    h = lax.axis_index("head")
    return d // 16, (h // 2) * 2 + d % 2, (d // 2) % 8, h % 2


def plane_peer(k):
    x, y, z, core = place()
    return device((x + k % 4) % 4, (y + k // 4) % 4, z, core)


def line_peer(k):
    x, y, z, core = place()
    return device(x, y, (z + k % 8) % 8, (core + k // 8) % 2)


def head_peer(k):
    h = lax.axis_index("head")
    return {"dp": lax.axis_index("dp"), "head": (h + k) % 4}


def send(src, dst, send_sem, recv_sem, peer):
    pltpu.make_async_remote_copy(
        src_ref=src, dst_ref=dst, send_sem=send_sem, recv_sem=recv_sem,
        device_id=peer, device_id_type=MESH,
    ).start()


def drain(ref, sem):
    pltpu.make_async_copy(ref, ref, sem).wait()


def each(lo, hi, body):
    def step(k, carry):
        body(k)
        return carry
    lax.fori_loop(lo, hi, step, 0)


def to_column(row):
    eye = lax.broadcasted_iota(jnp.int32, (128, 128), 0) == lax.broadcasted_iota(jnp.int32, (128, 128), 1)
    return jnp.concatenate(
        [jnp.sum(jnp.where(eye, row[:, 128 * k:128 * k + 128], 0.0), axis=1, keepdims=True)
         for k in range(row.shape[1] // 128)], axis=0)


def lse_rows(a):
    top = jnp.max(a, axis=0, keepdims=True)
    return top + jnp.log(jnp.sum(jnp.exp(a - top), axis=0, keepdims=True))


def put_stats(ref, lse, inv):
    for k in range(4):
        ref[k:k + 1, :] = lse[:, 128 * k:128 * k + 128]
    pick = lax.broadcasted_iota(jnp.int32, (32, 128), 0) == lax.broadcasted_iota(jnp.int32, (32, 128), 1)
    ref[4:5, :] = jnp.sum(jnp.where(pick, inv, 0.0), axis=0, keepdims=True)


def merged_stats(ref):
    a = ref[:, 0:4, :]
    top = jnp.max(a, axis=0)
    lse = top + jnp.log(jnp.sum(jnp.exp(a - top[None]), axis=0))
    lse = jnp.concatenate([lse[k:k + 1, :] for k in range(4)], axis=1)
    inv = jnp.concatenate([ref[k, 4:5, 0:32] for k in range(16)], axis=1)
    return lse, inv


def kernel(scale_ref, fi_ref, ft_ref, wi_ref, wt_ref, oi_ref, ot_ref,
           raw_s, raw_r, emb_i, emb_t, feat_i, feat_t, emb_it, emb_tt, feat_it, feat_tt,
           stat_i, stat_t, log_a, log_b, dem_i, dem_t, sib_s, sib_r, get_i, get_t,
           par_i, par_t, sum_i, sum_t, out_i, out_t, fin_i, fin_t, ssem, rsem):
    x, y, z, core = place()
    h = lax.axis_index("head")
    slot_i = y * 4 + x
    slot_t = core * 8 + z
    sibling = {"dp": lax.axis_index("dp"), "head": h + 1 - 2 * core}
    self_i = (y % 2) == core
    self_t = (y // 2) == (z // 4)

    bar = pltpu.get_barrier_semaphore()

    def hello(peer):
        pl.semaphore_signal(bar, inc=1, device_id=peer, device_id_type=MESH)

    each(1, 16, lambda k: hello(plane_peer(k)))
    each(1, 16, lambda k: hello(line_peer(k)))
    each(1, 4, lambda k: hello(head_peer(k)))

    def from_i(k):
        return device(k, (y // 2) * 2 + core, z, y % 2)

    def to_i(k):
        return device(k, (y // 2) * 2 + core, z, y % 2)

    def from_t(k):
        return device(x, (z // 4) * 2 + y % 2, (y // 2) * 4 + k, core)

    def to_t(k):
        return device(x, (z // 4) * 2 + y % 2, (y // 2) * 4 + k, core)

    def not_self(flag, k, mine, body):
        @pl.when(jnp.logical_not(flag & (k == mine)))
        def _():
            body()

    each(0, 4, lambda k: not_self(self_i, k, x, lambda: hello(from_i(k))))
    each(0, 4, lambda k: not_self(self_t, k, z % 4, lambda: hello(from_t(k))))

    raw_i = jnp.dot(fi_ref[...], wi_ref[...], preferred_element_type=F32)
    raw_t = jnp.dot(ft_ref[...], wt_ref[...], preferred_element_type=F32)
    for k in range(4):
        raw_s[k, 0:32, :] = raw_i[32 * k:32 * k + 32, :]
        raw_s[k, 32:64, :] = raw_t[32 * k:32 * k + 32, :]

    pl.semaphore_wait(bar, 41 - self_i.astype(jnp.int32) - self_t.astype(jnp.int32))

    def send_raw(k):
        peer = head_peer(k)
        send(raw_s.at[peer["head"]], raw_r.at[h], ssem.at[0], rsem.at[0], peer)

    each(1, 4, send_raw)
    raw_r[h] = raw_s[h]
    own = pl.ds(pl.multiple_of(h * 32, 32), 32)
    feat_i[pl.ds(pl.multiple_of(slot_i * 32, 32), 32), :] = fi_ref[own, :]
    feat_t[pl.ds(pl.multiple_of(slot_t * 32, 32), 32), :] = ft_ref[own, :]
    drain(raw_s.at[pl.ds(0, 3)], rsem.at[0])
    whole_i = jnp.concatenate([raw_r[k, 0:32, :] for k in range(4)], axis=1)
    whole_t = jnp.concatenate([raw_r[k, 32:64, :] for k in range(4)], axis=1)
    inv_i = lax.rsqrt(jnp.sum(whole_i * whole_i, axis=1, keepdims=True) + 1e-06)
    inv_t = lax.rsqrt(jnp.sum(whole_t * whole_t, axis=1, keepdims=True) + 1e-06)
    mine_i = pl.ds(pl.multiple_of(slot_i * 32, 32), 32)
    mine_t = pl.ds(pl.multiple_of(slot_t * 32, 32), 32)
    emb_i[mine_i, :] = (whole_i * inv_i).astype(BF16)
    emb_t[mine_t, :] = (whole_t * inv_t).astype(BF16)

    def spread(group, peer, ref, mine, sem):
        each(1, group, lambda k: send(ref.at[mine], ref.at[mine], ssem.at[sem], rsem.at[sem], peer(k)))

    half = pl.ds(pl.multiple_of(core * 256, 256), 256)
    other = pl.ds(pl.multiple_of((1 - core) * 256, 256), 256)
    spread(8, line_peer, emb_t, mine_t, 1)
    spread(16, plane_peer, emb_i, mine_i, 2)
    drain(emb_t.at[pl.ds(0, 224)], rsem.at[1])
    send(emb_t.at[half], emb_t.at[half], ssem.at[3], rsem.at[3], sibling)
    drain(emb_i.at[pl.ds(0, 480)], rsem.at[2])
    drain(emb_t.at[other], rsem.at[3])
    spread(8, line_peer, feat_t, mine_t, 4)
    spread(16, plane_peer, feat_i, mine_i, 5)

    scale = scale_ref[0, 0]
    nt = (((1,), (1,)), ((), ()))
    log_a[...] = scale * lax.dot_general(emb_i[...], emb_t[...], nt, preferred_element_type=F32)
    log_b[...] = scale * lax.dot_general(emb_t[...], emb_i[...], nt, preferred_element_type=F32)
    put_stats(stat_i.at[slot_i], lse_rows(log_b[...]), inv_i)
    put_stats(stat_t.at[slot_t], lse_rows(log_a[...]), inv_t)
    each(1, 16, lambda k: send(stat_i.at[slot_i], stat_i.at[slot_i], ssem.at[6], rsem.at[6], plane_peer(k)))
    each(1, 16, lambda k: send(stat_t.at[slot_t], stat_t.at[slot_t], ssem.at[7], rsem.at[7], line_peer(k)))
    emb_it[...] = emb_i[...].T
    emb_tt[...] = emb_t[...].T
    drain(stat_i.at[pl.ds(0, 15)], rsem.at[6])
    drain(stat_t.at[pl.ds(0, 15)], rsem.at[7])
    row_lse, invs_i = merged_stats(stat_i)
    col_lse, invs_t = merged_stats(stat_t)

    factor = 1.0 / (2.0 * (64.0 * 2.0 ** 0.5))
    ids0 = lax.broadcasted_iota(jnp.int32, (512, 512), 0)
    ids1 = lax.broadcasted_iota(jnp.int32, (512, 512), 1)
    nn = (((1,), (0,)), ((), ()))

    def grads(log, along, across, slot0, slot1, base, unit):
        a = log[...]
        same = (ids0 // 32 == slot0) & (ids0 - ids1 == 32 * (slot0 - slot1))
        g = (jnp.exp(a - along) + jnp.exp(a - across) - jnp.where(same, 2.0, 0.0)) * factor
        g = g.astype(BF16)
        inner = jnp.sum(g.astype(F32) * a, axis=0, keepdims=True)
        dem = scale * lax.dot_general(base[...], g, nn, preferred_element_type=F32)
        return (dem - unit[...].astype(F32) * inner).astype(BF16)

    dt = grads(log_a, to_column(row_lse), col_lse, slot_i, slot_t, emb_it, emb_tt)
    dem_t[...] = dt.reshape(2, 2, 256, 512)
    send(dem_t.at[:, 1 - core], sib_r, ssem.at[8], rsem.at[8], sibling)
    di = grads(log_b, row_lse, to_column(col_lse), slot_t, slot_i, emb_tt, emb_it)
    dem_i[...] = di.reshape(16, 64, 512)

    def send_i(k):
        peer = ((y + k // 4) % 4) * 4 + (x + k % 4) % 4
        send(dem_i.at[peer], get_i.at[slot_i], ssem.at[9], rsem.at[9], plane_peer(k))

    each(1, 16, send_i)
    get_i[slot_i] = dem_i[slot_i]
    drain(sib_r, rsem.at[8])
    sib_s[...] = (sib_r[...].astype(F32) + dem_t[:, core].astype(F32)).astype(BF16).reshape(8, 64, 512)

    def send_t(k):
        send(sib_s.at[(z + k) % 8], get_t.at[z], ssem.at[10], rsem.at[10], line_peer(k))

    each(1, 8, send_t)
    get_t[z] = sib_s[z]

    drain(feat_t.at[pl.ds(0, 224)], rsem.at[4])
    send(feat_t.at[half], feat_t.at[half], ssem.at[11], rsem.at[11], sibling)
    drain(feat_i.at[pl.ds(0, 480)], rsem.at[5])
    feat_it[...] = feat_i[...].T
    drain(feat_t.at[other], rsem.at[11])
    feat_tt[...] = feat_t[...].T

    drain(get_t.at[pl.ds(0, 7)], rsem.at[10])
    draw_t = (invs_t * jnp.sum(get_t[...].astype(F32), axis=0)).astype(BF16)
    out_t[...] = lax.dot_general(feat_tt[...], draw_t, nt, preferred_element_type=F32)
    for s in range(16):
        for a in range(2):
            rows = [320 * (s % 4) + 40 * (4 * (s // 8) + 2 * g + a) + 20 * ((s // 4) % 2) for g in range(2)]
            par_t[s, 24 * a:24 * a + 20, :] = jnp.concatenate([out_t[r:r + 20, :] for r in rows], axis=1)

    def part_t(k):
        peer = ((y + k // 4) % 4) * 4 + (x + k % 4) % 4
        send(par_t.at[peer], sum_t.at[slot_i], ssem.at[12], rsem.at[12], plane_peer(k))

    each(1, 16, part_t)
    sum_t[slot_i] = par_t[slot_i]

    drain(get_i.at[pl.ds(0, 15)], rsem.at[9])
    draw_i = (invs_i * jnp.sum(get_i[...].astype(F32), axis=0)).astype(BF16)
    out_i[...] = lax.dot_general(feat_it[...], draw_i, nt, preferred_element_type=F32)
    for q in range(16):
        for a in range(2):
            rows = [320 * (2 * g + a) + 40 * (q % 8) + 20 * (q // 8) for g in range(2)]
            par_i[q, 24 * a:24 * a + 20, :] = jnp.concatenate([out_i[r:r + 20, :] for r in rows], axis=1)

    def part_i(k):
        peer = ((core + k // 8) % 2) * 8 + (z + k % 8) % 8
        send(par_i.at[peer], sum_i.at[slot_t], ssem.at[13], rsem.at[13], line_peer(k))

    each(1, 16, part_i)
    sum_i[slot_t] = par_i[slot_t]

    def last(par, sums, fin, recv, flag, mine, slot, to, sem):
        drain(sums.at[pl.ds(0, 15)], recv)
        total = jnp.sum(sums[...], axis=0)
        for k in range(4):
            fin[0, k] = total[24 * (k % 2):24 * (k % 2) + 24, :]

        def one(k):
            not_self(flag, k, mine, lambda: send(fin.at[0, k], fin.at[1, slot], ssem.at[sem], rsem.at[sem], to(k)))

        each(0, 4, one)

        @pl.when(flag)
        def _():
            fin[1, slot] = fin[0, mine]

    def wait_last(fin, flag, sem):
        @pl.when(flag)
        def _():
            drain(fin.at[0, pl.ds(0, 3)], sem)

        @pl.when(jnp.logical_not(flag))
        def _():
            drain(fin.at[0], sem)

    last(par_t, sum_t, fin_t, rsem.at[12], self_t, z % 4, z % 4, to_t, 14)
    last(par_i, sum_i, fin_i, rsem.at[13], self_i, x, x, to_i, 15)

    def finish(o_ref, fin, flag, sem, half_id):
        wait_last(fin, flag, rsem.at[sem])
        for k in range(4):
            lo = fin[1, k, 0:20, 0:64]
            hi = fin[1, k, 0:20, 64:128]
            o_ref[:, 64 * k:64 * k + 64] = jnp.where(half_id == 0, lo, hi)

    finish(ot_ref, fin_t, self_t, 14, (z % 4) // 2)
    finish(oi_ref, fin_i, self_i, 15, x // 2)

    drain(raw_s.at[pl.ds(0, 3)], ssem.at[0])
    drain(emb_t.at[pl.ds(0, 224)], ssem.at[1])
    drain(emb_i.at[pl.ds(0, 480)], ssem.at[2])
    drain(emb_t.at[half], ssem.at[3])
    drain(feat_t.at[pl.ds(0, 224)], ssem.at[4])
    drain(feat_i.at[pl.ds(0, 480)], ssem.at[5])
    drain(stat_i.at[pl.ds(0, 15)], ssem.at[6])
    drain(stat_t.at[pl.ds(0, 15)], ssem.at[7])
    drain(sib_r, ssem.at[8])
    drain(get_i.at[pl.ds(0, 15)], ssem.at[9])
    drain(get_t.at[pl.ds(0, 7)], ssem.at[10])
    drain(feat_t.at[half], ssem.at[11])
    drain(sum_t.at[pl.ds(0, 15)], ssem.at[12])
    drain(sum_i.at[pl.ds(0, 15)], ssem.at[13])
    wait_last(fin_t, self_t, ssem.at[14])
    wait_last(fin_i, self_i, ssem.at[15])


def per_device(feat_img, feat_txt, w_img, w_txt, logit_scale):
    v = pl.BlockSpec(memory_space=pltpu.VMEM)
    out = jax.ShapeDtypeStruct((20, 256), F32)
    vm = pltpu.VMEM
    return pl.pallas_call(
        kernel,
        out_shape=(out, out),
        in_specs=[pl.BlockSpec(memory_space=pltpu.SMEM), v, v, v, v],
        out_specs=(v, v),
        scratch_shapes=[
            vm((4, 64, 256), F32), vm((4, 64, 256), F32),
            vm((512, 1024), BF16), vm((512, 1024), BF16),
            vm((512, 1280), BF16), vm((512, 1280), BF16),
            vm((1024, 512), BF16), vm((1024, 512), BF16),
            vm((1280, 512), BF16), vm((1280, 512), BF16),
            vm((16, 8, 128), F32), vm((16, 8, 128), F32),
            vm((512, 512), F32), vm((512, 512), F32),
            vm((16, 64, 512), BF16), vm((2, 2, 256, 512), BF16),
            vm((8, 64, 512), BF16), vm((2, 256, 512), BF16),
            vm((16, 64, 512), BF16), vm((8, 64, 512), BF16),
            vm((16, 48, 128), F32), vm((16, 48, 128), F32),
            vm((16, 48, 128), F32), vm((16, 48, 128), F32),
            vm((1280, 64), F32), vm((1280, 64), F32),
            vm((2, 4, 24, 128), F32), vm((2, 4, 24, 128), F32),
            pltpu.SemaphoreType.DMA((16,)), pltpu.SemaphoreType.DMA((16,)),
        ],
        compiler_params=pltpu.CompilerParams(
            collective_id=0, has_side_effects=True, vmem_limit_bytes=56 * 2 ** 20),
        name="contrastive",
    )(logit_scale.reshape(1, 1), feat_img, feat_txt, w_img, w_txt)


def solution(mesh):
    return jax.shard_map(
        per_device,
        mesh=mesh,
        in_specs=(P("dp", None), P("dp", None), P(None, "head"), P(None, "head"), P()),
        out_specs=(P("dp", "head"), P("dp", "head")),
        check_vma=False,
    )
```

```python
import jax
import jax.numpy as jnp
from jax import lax
from jax.experimental import pallas as pl
from jax.experimental.pallas import tpu as pltpu
from jax.sharding import PartitionSpec as P

MESH = pl.DeviceIdType.MESH
F32 = jnp.float32
BF16 = jnp.bfloat16
NT = (((1,), (1,)), ((), ()))
NN = (((1,), (0,)), ((), ()))


def device(x, y, z, core):
    x, y, z = (x + 4) % 4, (y + 4) % 4, (z + 8) % 8
    return {"dp": (x * 8 + z) * 2 + y % 2, "head": (y // 2) * 2 + core}


def place():
    d = lax.axis_index("dp")
    h = lax.axis_index("head")
    return d // 16, (h // 2) * 2 + d % 2, (d // 2) % 8, h % 2


def image_slot(x, y):
    x, y = (x + 4) % 4, (y + 4) % 4
    return (y % 2) * 8 + x * 2 + y // 2


def text_slot(z, core):
    z = (z + 8) % 8
    return (z // 4) * 8 + core * 4 + z % 4


def rows(slot, count=32, shift=0):
    return pl.ds(pl.multiple_of(slot * 32 + shift, 16), count)


def drain(ref, sem):
    pltpu.make_async_copy(ref, ref, sem).wait()


def each(lo, hi, body):
    def step(k, carry):
        body(k)
        return carry
    lax.fori_loop(lo, hi, step, 0)


def to_column(row):
    eye = lax.broadcasted_iota(jnp.int32, (128, 128), 0) == lax.broadcasted_iota(jnp.int32, (128, 128), 1)
    return jnp.concatenate(
        [jnp.sum(jnp.where(eye, row[:, 128 * k:128 * k + 128], 0.0), axis=1, keepdims=True)
         for k in range(row.shape[1] // 128)], axis=0)


def lse_rows(a):
    top = jnp.max(a, axis=0, keepdims=True)
    return top + jnp.log(jnp.sum(jnp.exp(a - top), axis=0, keepdims=True))


def put_stats(ref, lse, inv):
    for k in range(4):
        ref[k:k + 1, :] = lse[:, 128 * k:128 * k + 128]
    pick = lax.broadcasted_iota(jnp.int32, (32, 128), 0) == lax.broadcasted_iota(jnp.int32, (32, 128), 1)
    ref[4:5, :] = jnp.sum(jnp.where(pick, inv, 0.0), axis=0, keepdims=True)


def merged_stats(ref):
    a = ref[:, 0:4, :]
    top = jnp.max(a, axis=0)
    lse = top + jnp.log(jnp.sum(jnp.exp(a - top[None]), axis=0))
    lse = jnp.concatenate([lse[k:k + 1, :] for k in range(4)], axis=1)
    inv = jnp.concatenate([ref[k, 4:5, 0:32] for k in range(16)], axis=1)
    return lse, inv


def kernel(scale_ref, fi_ref, ft_ref, wi_ref, wt_ref, oi_ref, ot_ref,
           raw_s, raw_r, emb_i, emb_t, feat_i, feat_t, emb_it, emb_tt, feat_it, feat_tt,
           stat_i, stat_t, log_a, log_b, dem_i, dem_t, sib_s, sib_r, get_i, get_t,
           par_i, par_t, sum_i, sum_t, out_s, out_r, fin_i, fin_t, ssem, rsem):
    x, y, z, core = place()
    h = lax.axis_index("head")
    slot_i = image_slot(x, y)
    slot_t = text_slot(z, core)
    sibling = device(x, y, z, 1 - core)
    due = {}
    sent = {}

    def send(src, dst, sem, peer, arrival=None):
        pltpu.make_async_remote_copy(
            src_ref=src, dst_ref=dst, send_sem=ssem.at[sem], recv_sem=rsem.at[sem if arrival is None else arrival],
            device_id=peer, device_id_type=MESH,
        ).start()

    def arrive(i):
        drain(due.pop(i), rsem.at[i])

    def head_peer(k):
        return {"dp": lax.axis_index("dp"), "head": (h + k) % 4}

    def plane_peer(k):
        return device(x + k % 4, y + k // 4, z, core)

    def line_peer(k):
        return device(x, y, z + k % 8, (core + k // 8) % 2)

    self_i = (z % 2 == x // 2) & (core == x % 2) & (core == x // 2)
    self_t = (y == z // 2) & (core == y // 2) & ((z % 4) // 2 == core)
    quarter = (z % 2) * 2 + y % 2

    def to_i(e):
        return device((z % 2) * 2 + core, (y // 2) * 2 + e % 2, (z // 2) * 2 + e // 2, x // 2)

    def to_t(e):
        return device(x, core * 2 + e % 2, 2 * y + e // 2, (z % 4) // 2)

    bar = pltpu.get_barrier_semaphore()

    def hello(peer):
        pl.semaphore_signal(bar, inc=1, device_id=peer, device_id_type=MESH)

    each(1, 4, lambda k: hello(head_peer(k)))
    each(1, 4, lambda k: hello(device(x + k, y, z, core)))
    hello(device(x, y + 1, z, core))
    hello(device(x, y - 1, z, core))
    each(1, 4, lambda k: hello(device(x, y, z + k, core)))
    each(1, 4, lambda k: hello(device(x, y, z - k, core)))

    raw_i = jnp.dot(fi_ref[...].reshape(128, 1280), wi_ref[...], preferred_element_type=F32)
    for k in range(4):
        raw_s[0, k] = raw_i[32 * k:32 * k + 32, :]
    raw_t = jnp.dot(ft_ref[...].reshape(128, 1280), wt_ref[...], preferred_element_type=F32)
    for k in range(4):
        raw_s[1, k] = raw_t[32 * k:32 * k + 32, :]

    pl.semaphore_wait(bar, 14)

    def send_raw(side, sem):
        def one(k):
            peer = head_peer(k)
            send(raw_s.at[side, peer["head"]], raw_r.at[side, h], sem, peer)
        each(1, 4, one)
        due[sem] = sent[sem] = raw_s.at[side, pl.ds(0, 3)]
        raw_r[side, h] = raw_s[side, h]

    send_raw(0, 0)
    send_raw(1, 1)

    each(1, 4, lambda k: send(fi_ref.at[:, core], feat_i.at[x], 2, device(x + k, y, z, core)))
    due[2] = sent[2] = feat_i.at[pl.ds(0, 3)]
    feat_i[x] = fi_ref[:, core]
    each(1, 4, lambda k: send(ft_ref.at[y // 2, core], feat_t.at[core, z % 4], 3,
                              device(x, y, (z // 4) * 4 + (z + k) % 4, core)))
    due[3] = sent[3] = feat_t.at[0, pl.ds(0, 3)]
    feat_t[core, z % 4] = ft_ref[y // 2, core]

    def unit_rows(side):
        whole = jnp.concatenate([raw_r[side, k] for k in range(4)], axis=1)
        inv = lax.rsqrt(jnp.sum(whole * whole, axis=1, keepdims=True) + 1e-06)
        return (whole * inv).astype(BF16), inv

    order = (1, 3, 2)
    mine_i = rows(slot_i)
    mine_t = rows(slot_t)
    arrive(0)
    unit_i, inv_i = unit_rows(0)
    emb_i[mine_i, :] = unit_i
    for k in order:
        send(emb_i.at[mine_i], emb_i.at[mine_i], 4, device(x + k, y, z, core), 4 + k)
        send(emb_i.at[mine_i], emb_i.at[mine_i], 4, device(x, y + k, z, core), 7 + k)
        due[4 + k] = due[7 + k] = emb_i.at[rows(0)]
    sent[4] = emb_i.at[rows(0, 480)]
    due[11] = emb_i.at[rows(0, 288)]
    arrive(1)
    unit_t, inv_t = unit_rows(1)
    emb_t[mine_t, :] = unit_t
    for k, s in enumerate((2, -2, 1, -1)):
        send(emb_t.at[mine_t], emb_t.at[mine_t], 12, device(x, y, z + s, core), 12 + k)
        due[12 + k] = emb_t.at[rows(0)]
    sent[12] = emb_t.at[rows(0, 224)]
    due[16] = emb_t.at[rows(0, 96)]

    def forward_x(k):
        arrive(4 + k)
        block = rows(image_slot(x - k, y), 16)
        for j in order:
            send(emb_i.at[block], emb_i.at[block], 4, device(x, y + j, z, core), 11)

    def forward_y(k):
        arrive(7 + k)
        block = rows(image_slot(x, y - k), 16, 16)
        for j in order:
            send(emb_i.at[block], emb_i.at[block], 4, device(x + j, y, z, core), 11)

    def forward_z(k, s):
        arrive(12 + k)
        block = rows(text_slot(z + 2 * s, core))
        send(emb_t.at[block], emb_t.at[block], 12, device(x, y, z - s, core), 16)
        block = rows(text_slot(z + 2 * s, core), 16, 16 * k)
        send(emb_t.at[block], emb_t.at[block], 12, device(x, y, z - 2 * s, core), 16)

    forward_x(1)
    forward_y(1)
    forward_x(3)
    forward_y(3)
    forward_x(2)
    forward_y(2)
    forward_z(0, -1)
    forward_z(1, 1)
    arrive(14)
    arrive(15)
    arrive(16)
    for k in range(2):
        part = pl.ds(pl.multiple_of(256 * k + 128 * core, 128), 128)
        send(emb_t.at[part], emb_t.at[part], 17, sibling)
    due[17] = sent[17] = emb_t.at[pl.ds(0, 256)]
    arrive(11)
    arrive(17)

    scale = scale_ref[0, 0]
    log_a[...] = scale * lax.dot_general(emb_i[...], emb_t[...], NT, preferred_element_type=F32)
    log_b[...] = scale * lax.dot_general(emb_t[...], emb_i[...], NT, preferred_element_type=F32)
    put_stats(stat_i.at[slot_i], lse_rows(log_b[...]), inv_i)
    put_stats(stat_t.at[slot_t], lse_rows(log_a[...]), inv_t)
    each(1, 16, lambda k: send(stat_i.at[slot_i], stat_i.at[slot_i], 18, plane_peer(k)))
    due[18] = sent[18] = stat_i.at[pl.ds(0, 15)]
    each(1, 16, lambda k: send(stat_t.at[slot_t], stat_t.at[slot_t], 19, line_peer(k)))
    due[19] = sent[19] = stat_t.at[pl.ds(0, 15)]
    emb_it[...] = emb_i[...].T
    emb_tt[...] = emb_t[...].T
    arrive(3)
    send(feat_t.at[core], feat_t.at[core], 20, sibling)
    due[20] = sent[20] = feat_t.at[0]
    arrive(2)
    feat_it[...] = feat_i[...].reshape(256, 1280).T
    arrive(18)
    arrive(19)
    row_lse, invs_i = merged_stats(stat_i)
    col_lse, invs_t = merged_stats(stat_t)

    factor = 1.0 / (2.0 * (64.0 * 2.0 ** 0.5))
    ids0 = lax.broadcasted_iota(jnp.int32, (512, 512), 0)
    ids1 = lax.broadcasted_iota(jnp.int32, (512, 512), 1)

    def grads(log, along, across, slot0, slot1, base, unit, dem):
        a = log[...]
        same = (ids0 // 32 == slot0) & (ids0 - ids1 == 32 * (slot0 - slot1))
        g = (jnp.exp(a - along) + jnp.exp(a - across) - jnp.where(same, 2.0, 0.0)) * factor
        g = g.astype(BF16)
        inner = jnp.sum(g.astype(F32) * a, axis=0, keepdims=True)
        d = scale * lax.dot_general(base[...], g, NN, preferred_element_type=F32)
        d = (d - unit[...].astype(F32) * inner).astype(BF16)
        for k in range(2):
            dem[k] = d[:, 256 * k:256 * k + 256].reshape(8, 128, 256)

    grads(log_a, to_column(row_lse), col_lse, slot_i, slot_t, emb_it, emb_tt, dem_t)
    send(dem_t.at[:, pl.ds(4 - 4 * core, 4)], sib_r, 21, sibling)
    due[21] = sent[21] = sib_r
    grads(log_b, row_lse, to_column(col_lse), slot_t, slot_i, emb_tt, emb_it, dem_i)

    def send_i(k):
        px, py = (x + k % 4) % 4, (y + k // 4) % 4
        send(dem_i.at[py % 2, (py // 2) * 4 + px], get_i.at[slot_i], 22, plane_peer(k))

    each(1, 16, send_i)
    due[22] = sent[22] = get_i.at[pl.ds(0, 15)]
    get_i[slot_i] = dem_i[y % 2, (y // 2) * 4 + x]
    arrive(21)
    own = dem_t[:, pl.ds(4 * core, 4)]
    sib_s[...] = (sib_r[...].astype(F32) + own.astype(F32)).astype(BF16).reshape(8, 128, 256)

    def send_t(k):
        send(sib_s.at[(z + k) % 8], get_t.at[z], 23, line_peer(k))

    each(1, 8, send_t)
    due[23] = sent[23] = get_t.at[pl.ds(0, 7)]
    get_t[z] = sib_s[z]
    arrive(20)
    feat_tt[...] = feat_t[...].reshape(256, 1280).T

    def weights(get, invs, upper, feats):
        inv = jnp.where(upper, invs[:, 256:512], invs[:, 0:256])
        draw = inv * jnp.sum(get[...].astype(F32), axis=0)
        high = draw.astype(BF16)
        low = (draw - high.astype(F32)).astype(BF16)
        f = feats[...]
        out = lax.dot_general(f, high, NT, preferred_element_type=F32)
        out += lax.dot_general(f, low, NT, preferred_element_type=F32)
        return out.reshape(16, 80, 128)

    arrive(23)
    par_t[...] = weights(get_t, invs_t, z // 4 == 1, feat_tt).astype(BF16)

    def part_t(k):
        px, py = (x + k % 4) % 4, (y + k // 4) % 4
        send(par_t.at[px * 4 + py], sum_t.at[slot_i], 24, plane_peer(k))

    each(1, 16, part_t)
    due[24] = sent[24] = sum_t.at[pl.ds(0, 15)]
    sum_t[slot_i] = par_t[x * 4 + y]

    arrive(22)
    def chunk_i(pz, pc):
        return ((pz % 2) * 2 + pc) * 4 + pz // 2

    par_i[...] = weights(get_i, invs_i, y % 2 == 1, feat_it)
    for k in range(8):
        out_s[k] = par_i[chunk_i(k, 1 - core)]
    send(out_s, out_r, 25, sibling)
    due[25] = sent[25] = out_r
    arrive(25)
    for k in range(8):
        par_t_i = par_i[chunk_i(k, core)] + out_r[k]
        sib_p = par_t_i.astype(BF16)
        sum_i[8 + k] = sib_p

    def part_i(k):
        send(sum_i.at[8 + (z + k) % 8], sum_i.at[z], 26, line_peer(k))

    each(1, 8, part_i)
    due[26] = sent[26] = sum_i.at[pl.ds(0, 7)]
    sum_i[z] = sum_i[8 + z]

    def last(total, fin, flag, slot, to, sem):
        for k in range(4):
            fin[0, k, 0:20, :] = total[20 * k:20 * k + 20, :]

        def one(k):
            @pl.when(jnp.logical_not(flag & (k == quarter)))
            def _():
                send(fin.at[0, k], fin.at[1, slot], sem, to(k))

        each(0, 4, one)

        @pl.when(flag)
        def _():
            fin[1, slot] = fin[0, quarter]

    def wait_last(fin, flag, sem):
        @pl.when(flag)
        def _():
            drain(fin.at[0, pl.ds(0, 3)], sem)

        @pl.when(jnp.logical_not(flag))
        def _():
            drain(fin.at[0], sem)

    arrive(24)
    last(jnp.sum(sum_t[...].astype(F32), axis=0), fin_t, self_t, (z // 4) * 2 + z % 2, to_t, 27)
    arrive(26)
    last(jnp.sum(sum_i[0:8].astype(F32), axis=0), fin_i, self_i, (y % 2) * 2 + x % 2, to_i, 28)

    def finish(o_ref, fin, flag, sem):
        wait_last(fin, flag, rsem.at[sem])
        for k in range(2):
            o_ref[:, 128 * k:128 * k + 128] = fin[1, k, 0:20, :] + fin[1, 2 + k, 0:20, :]

    finish(ot_ref, fin_t, self_t, 27)
    finish(oi_ref, fin_i, self_i, 28)

    for i, ref in sent.items():
        drain(ref, ssem.at[i])
    wait_last(fin_t, self_t, ssem.at[27])
    wait_last(fin_i, self_i, ssem.at[28])


def per_device(feat_img, feat_txt, w_img, w_txt, logit_scale):
    v = pl.BlockSpec(memory_space=pltpu.VMEM)
    out = jax.ShapeDtypeStruct((20, 256), F32)
    vm = pltpu.VMEM
    return pl.pallas_call(
        kernel,
        out_shape=(out, out),
        in_specs=[pl.BlockSpec(memory_space=pltpu.SMEM), v, v, v, v],
        out_specs=(v, v),
        scratch_shapes=[
            vm((2, 4, 32, 256), F32), vm((2, 4, 32, 256), F32),
            vm((512, 1024), BF16), vm((512, 1024), BF16),
            vm((4, 2, 32, 1280), BF16), vm((2, 4, 32, 1280), BF16),
            vm((1024, 512), BF16), vm((1024, 512), BF16),
            vm((1280, 256), BF16), vm((1280, 256), BF16),
            vm((16, 8, 128), F32), vm((16, 8, 128), F32),
            vm((512, 512), F32), vm((512, 512), F32),
            vm((2, 8, 128, 256), BF16), vm((2, 8, 128, 256), BF16),
            vm((8, 128, 256), BF16), vm((2, 4, 128, 256), BF16),
            vm((16, 128, 256), BF16), vm((8, 128, 256), BF16),
            vm((16, 80, 128), F32), vm((16, 80, 128), BF16),
            vm((16, 80, 128), BF16), vm((16, 80, 128), BF16),
            vm((8, 80, 128), F32), vm((8, 80, 128), F32),
            vm((2, 4, 24, 128), F32), vm((2, 4, 24, 128), F32),
            pltpu.SemaphoreType.DMA((32,)), pltpu.SemaphoreType.DMA((32,)),
        ],
        compiler_params=pltpu.CompilerParams(
            collective_id=0, has_side_effects=True, vmem_limit_bytes=56 * 2 ** 20),
        name="contrastive",
    )(logit_scale.reshape(1, 1), feat_img.reshape(2, 2, 32, 1280), feat_txt.reshape(2, 2, 32, 1280), w_img, w_txt)


def solution(mesh):
    return jax.shard_map(
        per_device,
        mesh=mesh,
        in_specs=(P("dp", None), P("dp", None), P(None, "head"), P(None, "head"), P()),
        out_specs=(P("dp", "head"), P("dp", "head")),
        check_vma=False,
    )
```

```python
import jax
import jax.numpy as jnp
from jax import lax
from jax.experimental import pallas as pl
from jax.experimental.pallas import tpu as pltpu
from jax.sharding import PartitionSpec as P

MESH = pl.DeviceIdType.MESH
F32 = jnp.float32
BF16 = jnp.bfloat16
NT = (((1,), (1,)), ((), ()))
NN = (((1,), (0,)), ((), ()))


def device(x, y, z, core):
    x, y, z = (x + 4) % 4, (y + 4) % 4, (z + 8) % 8
    return {"dp": (x * 8 + z) * 2 + y % 2, "head": (y // 2) * 2 + core}


def place():
    d = lax.axis_index("dp")
    h = lax.axis_index("head")
    return d // 16, (h // 2) * 2 + d % 2, (d // 2) % 8, h % 2


def image_slot(x, y):
    x, y = (x + 4) % 4, (y + 4) % 4
    return (y % 2) * 8 + x * 2 + y // 2


def text_slot(z, core):
    z = (z + 8) % 8
    return (z // 4) * 8 + core * 4 + z % 4


def rows(slot, count=32, shift=0):
    return pl.ds(pl.multiple_of(slot * 32 + shift, 16), count)


def drain(ref, sem):
    pltpu.make_async_copy(ref, ref, sem).wait()


def each(lo, hi, body):
    def step(k, carry):
        body(k)
        return carry
    lax.fori_loop(lo, hi, step, 0)


def to_column(row):
    eye = lax.broadcasted_iota(jnp.int32, (128, 128), 0) == lax.broadcasted_iota(jnp.int32, (128, 128), 1)
    return jnp.concatenate(
        [jnp.sum(jnp.where(eye, row[:, 128 * k:128 * k + 128], 0.0), axis=1, keepdims=True)
         for k in range(row.shape[1] // 128)], axis=0)


def lse_rows(a):
    top = jnp.max(a, axis=0, keepdims=True)
    return top + jnp.log(jnp.sum(jnp.exp(a - top), axis=0, keepdims=True))


def put_stats(ref, lse, inv):
    for k in range(4):
        ref[k:k + 1, :] = lse[:, 128 * k:128 * k + 128]
    pick = lax.broadcasted_iota(jnp.int32, (32, 128), 0) == lax.broadcasted_iota(jnp.int32, (32, 128), 1)
    ref[4:5, :] = jnp.sum(jnp.where(pick, inv, 0.0), axis=0, keepdims=True)


def merged_stats(ref):
    a = ref[:, 0:4, :]
    top = jnp.max(a, axis=0)
    lse = top + jnp.log(jnp.sum(jnp.exp(a - top[None]), axis=0))
    lse = jnp.concatenate([lse[k:k + 1, :] for k in range(4)], axis=1)
    inv = jnp.concatenate([ref[k, 4:5, 0:32] for k in range(16)], axis=1)
    return lse, inv


def kernel(scale_ref, fi_ref, ft_ref, wi_ref, wt_ref, oi_ref, ot_ref,
           fi_v, ft_v, wi_v, wt_v,
           raw_s, raw_r, emb_i, emb_t, feat_i, feat_t, emb_it, emb_tt, feat_it, feat_tt,
           stat_i, stat_t, log_a, log_b, own_i, dem_x, dem_y, get_x, get_y, dem_x2, dem_y2, last_x, last_y,
           own_t, dem_t, sib_r, sib_s, full_z, half_z, sum_z, get_t,
           par_i, par_t, sum_i, sum_t, out_s, out_r, fin_i, fin_t, ssem, rsem, lsem):
    x, y, z, core = place()
    h = lax.axis_index("head")
    slot_i = image_slot(x, y)
    slot_t = text_slot(z, core)
    sibling = device(x, y, z, 1 - core)
    due = {}
    sent = {}

    def send(src, dst, sem, peer, arrival=None):
        pltpu.make_async_remote_copy(
            src_ref=src, dst_ref=dst, send_sem=ssem.at[sem], recv_sem=rsem.at[sem if arrival is None else arrival],
            device_id=peer, device_id_type=MESH,
        ).start()

    def arrive(i):
        drain(due.pop(i), rsem.at[i])

    def head_peer(k):
        return {"dp": lax.axis_index("dp"), "head": (h + k) % 4}

    def plane_peer(k):
        return device(x + k % 4, y + k // 4, z, core)

    def line_peer(k):
        return device(x, y, z + k % 8, (core + k // 8) % 2)

    self_i = (z % 2 == x // 2) & (core == x % 2) & (core == x // 2)
    self_t = (y == z // 2) & (core == y // 2) & ((z % 4) // 2 == core)
    quarter = (z % 2) * 2 + y % 2

    def to_i(e):
        return device((z % 2) * 2 + core, (y // 2) * 2 + e % 2, (z // 2) * 2 + e // 2, x // 2)

    def to_t(e):
        return device(x, core * 2 + e % 2, 2 * y + e // 2, (z % 4) // 2)

    bar = pltpu.get_barrier_semaphore()

    def hello(peer):
        pl.semaphore_signal(bar, inc=1, device_id=peer, device_id_type=MESH)

    each(1, 4, lambda k: hello(head_peer(k)))
    each(1, 4, lambda k: hello(device(x + k, y, z, core)))
    hello(device(x, y + 1, z, core))
    hello(device(x, y - 1, z, core))
    each(1, 4, lambda k: hello(device(x, y, z + k, core)))
    each(1, 4, lambda k: hello(device(x, y, z - k, core)))

    fetched = [pltpu.make_async_copy(a, b, lsem.at[k])
               for k, (a, b) in enumerate(((fi_ref, fi_v), (wi_ref, wi_v), (ft_ref, ft_v), (wt_ref, wt_v)))]
    for copy in fetched:
        copy.start()

    for side, (f, w) in enumerate(((fi_v, wi_v), (ft_v, wt_v))):
        fetched[2 * side].wait()
        fetched[2 * side + 1].wait()
        raw = jnp.dot(f[...].reshape(128, 1280), w[...], preferred_element_type=F32)
        raw_s[side] = raw.reshape(4, 32, 256)

    pl.semaphore_wait(bar, 14)

    def send_raw(side, sem):
        def one(k):
            peer = head_peer(k)
            send(raw_s.at[side, peer["head"]], raw_r.at[side, h], sem, peer)
        each(1, 4, one)
        due[sem] = sent[sem] = raw_s.at[side, pl.ds(0, 3)]
        raw_r[side, h] = raw_s[side, h]

    send_raw(0, 0)
    send_raw(1, 1)

    def unit_rows(side):
        whole = jnp.concatenate([raw_r[side, k] for k in range(4)], axis=1)
        inv = lax.rsqrt(jnp.sum(whole * whole, axis=1, keepdims=True) + 1e-06)
        return (whole * inv).astype(BF16), inv

    order = (1, 3, 2)
    mine_i = rows(slot_i)
    mine_t = rows(slot_t)
    arrive(0)
    unit_i, inv_i = unit_rows(0)
    emb_i[mine_i, :] = unit_i
    for k in order:
        send(emb_i.at[mine_i], emb_i.at[mine_i], 4, device(x + k, y, z, core), 4 + k)
        send(emb_i.at[mine_i], emb_i.at[mine_i], 4, device(x, y + k, z, core), 7 + k)
        due[4 + k] = due[7 + k] = emb_i.at[rows(0)]
    arrive(1)
    unit_t, inv_t = unit_rows(1)
    emb_t[mine_t, :] = unit_t
    for k, s in enumerate((2, -2, 1, -1)):
        send(emb_t.at[mine_t], emb_t.at[mine_t], 12, device(x, y, z + s, core), 12 + k)
        due[12 + k] = emb_t.at[rows(0)]

    def forward_x(k):
        arrive(4 + k)
        block = rows(image_slot(x - k, y), 16)
        for j in order:
            send(emb_i.at[block], emb_i.at[block], 4, device(x, y + j, z, core), 11)

    def forward_y(k):
        arrive(7 + k)
        block = rows(image_slot(x, y - k), 16, 16)
        for j in order:
            send(emb_i.at[block], emb_i.at[block], 4, device(x + j, y, z, core), 11)

    def forward_z(k, s):
        arrive(12 + k)
        block = rows(text_slot(z + 2 * s, core))
        send(emb_t.at[block], emb_t.at[block], 12, device(x, y, z - s, core), 16)
        block = rows(text_slot(z + 2 * s, core), 16, 16 * k)
        send(emb_t.at[block], emb_t.at[block], 12, device(x, y, z - 2 * s, core), 16)

    def to_sibling(z_from):
        block = rows(text_slot(z_from, core))
        send(emb_t.at[block], emb_t.at[block], 17, sibling)

    to_sibling(z)
    forward_x(1)
    forward_y(1)
    forward_x(3)
    forward_y(3)
    forward_z(0, -1)
    forward_z(1, 1)
    forward_x(2)
    forward_y(2)
    due[11] = emb_i.at[rows(0, 288)]
    due[16] = emb_t.at[rows(0, 96)]
    sent[4] = emb_i.at[rows(0, 480)]
    sent[12] = emb_t.at[rows(0, 224)]
    to_sibling(z - 2)
    to_sibling(z + 2)
    arrive(14)
    to_sibling(z - 1)
    arrive(15)
    to_sibling(z + 1)
    arrive(16)
    to_sibling(z + 3)
    to_sibling(z - 3)
    to_sibling(z + 4)
    due[17] = sent[17] = emb_t.at[pl.ds(0, 256)]
    arrive(11)
    arrive(17)

    scale = scale_ref[0, 0]
    log_a[...] = scale * lax.dot_general(emb_i[...], emb_t[...], NT, preferred_element_type=F32)
    log_b[...] = scale * lax.dot_general(emb_t[...], emb_i[...], NT, preferred_element_type=F32)
    put_stats(stat_i.at[slot_i], lse_rows(log_b[...]), inv_i)
    put_stats(stat_t.at[slot_t], lse_rows(log_a[...]), inv_t)
    each(1, 16, lambda k: send(stat_i.at[slot_i], stat_i.at[slot_i], 18, plane_peer(k)))
    due[18] = sent[18] = stat_i.at[pl.ds(0, 15)]
    each(1, 16, lambda k: send(stat_t.at[slot_t], stat_t.at[slot_t], 19, line_peer(k)))
    due[19] = sent[19] = stat_t.at[pl.ds(0, 15)]
    each(1, 4, lambda k: send(fi_v.at[:, core], feat_i.at[x], 2, device(x + k, y, z, core)))
    due[2] = sent[2] = feat_i.at[pl.ds(0, 3)]
    feat_i[x] = fi_v[:, core]
    each(1, 4, lambda k: send(ft_v.at[y // 2, core], feat_t.at[core, z % 4], 3,
                              device(x, y, (z // 4) * 4 + (z + k) % 4, core)))
    due[3] = sent[3] = feat_t.at[0, pl.ds(0, 3)]
    feat_t[core, z % 4] = ft_v[y // 2, core]

    emb_it[...] = emb_i[...].T
    emb_tt[...] = emb_t[...].T
    arrive(18)
    arrive(19)
    row_lse, invs_i = merged_stats(stat_i)
    col_lse, invs_t = merged_stats(stat_t)

    factor = 1.0 / (2.0 * (64.0 * 2.0 ** 0.5))
    ids0 = lax.broadcasted_iota(jnp.int32, (512, 512), 0)
    ids1 = lax.broadcasted_iota(jnp.int32, (512, 512), 1)

    def grads(log, along, across, slot0, slot1):
        a = log[...]
        same = (ids0 // 32 == slot0) & (ids0 - ids1 == 32 * (slot0 - slot1))
        g = (jnp.exp(a - along) + jnp.exp(a - across) - jnp.where(same, 2.0, 0.0)) * factor
        g = g.astype(BF16)
        return g, jnp.sum(g.astype(F32) * a, axis=0, keepdims=True)

    def demb(g, inner, base, unit, half):
        part = pl.ds(pl.multiple_of(512 * half, 512), 512)
        d = scale * lax.dot_general(base[part, :], g, NN, preferred_element_type=F32)
        return d - unit[part, :].astype(F32) * inner

    g, inner = grads(log_a, to_column(row_lse), col_lse, slot_i, slot_t)
    d = demb(g, inner, emb_it, emb_tt, 1 - core)
    for k in range(2):
        dem_t[k] = d[:, 256 * k:256 * k + 256].astype(BF16).reshape(4, 128, 256)
    send(dem_t, sib_r, 21, sibling)
    due[21] = sent[21] = sib_r
    d = demb(g, inner, emb_it, emb_tt, core)
    for k in range(2):
        own_t[4 * k:4 * k + 4] = d[:, 256 * k:256 * k + 256].reshape(4, 128, 256)

    g, inner = grads(log_b, row_lse, to_column(col_lse), slot_t, slot_i)

    def image_half(pair):
        d = demb(g, inner, emb_tt, emb_it, pair)
        for k in range(2):
            py = 2 * pair + k
            e = d[:, 256 * k:256 * k + 256].reshape(4, 2, 64, 256)
            own_i[py] = e
            dem_x[:, py] = e[:, 0].astype(BF16)
            dem_y[py] = e[:, 1].astype(BF16)

    def send_y(py):
        send(dem_y.at[py], get_y.at[y], 29, device(x, py, z, core))

    image_half(1 - y // 2)
    send_y((y + 2) % 4)
    send_y((1 - y // 2) * 2 + (y + 1) % 2)
    image_half(y // 2)
    each(0, 3, lambda k: send(dem_x.at[(x + 1 + (k + 1) % 3) % 4], get_x.at[x], 22, device(x + 1 + (k + 1) % 3, y, z, core)))
    send_y((y // 2) * 2 + (y + 1) % 2)
    due[22] = sent[22] = get_x.at[pl.ds(0, 3)]
    due[29] = sent[29] = get_y.at[pl.ds(0, 3)]
    arrive(21)
    own_t[...] = own_t[...] + sib_r[...].astype(F32).reshape(8, 128, 256)
    sib_s[...] = own_t[...].astype(BF16)
    for k, s in enumerate((1, -1)):
        far = (z + 4) % 8
        half = pl.ds(64 * k, 64)
        send(sib_s.at[far, half], half_z.at[k], 30, device(x, y, z + 2 * s, core))
        send(sib_s.at[(z + 3 * s + 8) % 8], full_z.at[k], 23, device(x, y, z + s, core))
        send(sib_s.at[(z + s + 8) % 8], get_t.at[k], 31, device(x, y, z + s, core))
    due[23] = sent[23] = full_z
    due[30] = sent[30] = half_z

    arrive(3)
    send(feat_t.at[core], feat_t.at[core], 20, sibling)
    due[20] = sent[20] = feat_t.at[0]
    arrive(2)
    feat_it[...] = feat_i[...].reshape(256, 1280).T
    arrive(20)
    feat_tt[...] = feat_t[...].reshape(256, 1280).T

    arrive(29)
    for k in range(1, 4):
        px = (x + k) % 4
        total = own_i[y, px, 1]
        for j in range(1, 4):
            total += get_y[(y + j) % 4, px].astype(F32)
        dem_y2[px] = total.astype(BF16)
        send(dem_y2.at[px], last_y.at[x], 32, device(px, y, z, core))
    due[32] = sent[32] = last_y.at[pl.ds(0, 3)]
    arrive(22)
    for k in range(1, 4):
        py = (y + k) % 4
        total = own_i[py, x, 0]
        for j in range(1, 4):
            total += get_x[(x + j) % 4, py].astype(F32)
        dem_x2[py] = total.astype(BF16)
        send(dem_x2.at[py], last_x.at[y], 33, device(x, py, z, core))
    due[33] = sent[33] = last_x.at[pl.ds(0, 3)]
    arrive(23)
    arrive(30)
    for k, s in enumerate((1, -1)):
        dest = (z + 2 * s + 8) % 8
        total = own_t[dest] + full_z[k].astype(F32)
        extra = half_z[k].astype(F32)
        blank = jnp.zeros_like(extra)
        total += jnp.concatenate([extra, blank] if k == 0 else [blank, extra], axis=0)
        sum_z[k] = total.astype(BF16)
        send(sum_z.at[k], get_t.at[2 + k], 31, device(x, y, z + 2 * s, core))
    due[31] = sent[31] = get_t

    def weights(total, invs, upper, feats):
        inv = jnp.where(upper, invs[:, 256:512], invs[:, 0:256])
        draw = inv * total
        high = draw.astype(BF16)
        low = (draw - high.astype(F32)).astype(BF16)
        f = feats[...]
        out = lax.dot_general(f, high, NT, preferred_element_type=F32)
        out += lax.dot_general(f, low, NT, preferred_element_type=F32)
        return out.reshape(16, 80, 128)

    def image_sum(own, first, lines, last, at):
        total = own
        for j in range(1, 4):
            total += first((at + j) % 4).astype(F32)
            total += last[(lines + j) % 4].astype(F32)
        return total

    arrive(32)
    arrive(33)
    def chunk_i(pz, pc):
        return ((pz % 2) * 2 + pc) * 4 + pz // 2

    upper_cols = image_sum(own_i[y, x, 0], lambda j: get_x[j, y], y, last_x, x)
    lower_cols = image_sum(own_i[y, x, 1], lambda j: get_y[j, x], x, last_y, y)
    total_i = jnp.concatenate([upper_cols, lower_cols], axis=0)
    par_i[...] = weights(total_i, invs_i, y % 2 == 1, feat_it)
    for k in range(8):
        out_s[k] = par_i[chunk_i(k, 1 - core)]
    send(out_s, out_r, 25, sibling)
    due[25] = sent[25] = out_r
    arrive(25)
    for k in range(8):
        par_t_i = par_i[chunk_i(k, core)] + out_r[k]
        sib_p = par_t_i.astype(BF16)
        sum_i[8 + k] = sib_p

    def part_i(k):
        send(sum_i.at[8 + (z + k) % 8], sum_i.at[z], 26, line_peer(k))

    each(1, 8, part_i)
    due[26] = sent[26] = sum_i.at[pl.ds(0, 7)]
    sum_i[z] = sum_i[8 + z]


    arrive(31)
    total_t = own_t[z] + jnp.sum(get_t[...].astype(F32), axis=0)
    par_t[...] = weights(total_t, invs_t, z // 4 == 1, feat_tt).astype(BF16)

    def part_t(k):
        px, py = (x + k % 4) % 4, (y + k // 4) % 4
        send(par_t.at[px * 4 + py], sum_t.at[slot_i], 24, plane_peer(k))

    each(1, 16, part_t)
    due[24] = sent[24] = sum_t.at[pl.ds(0, 15)]
    sum_t[slot_i] = par_t[x * 4 + y]
    def last(total, fin, flag, slot, to, sem):
        for k in range(4):
            fin[0, k, 0:20, :] = total[20 * k:20 * k + 20, :]

        def one(k):
            @pl.when(jnp.logical_not(flag & (k == quarter)))
            def _():
                send(fin.at[0, k], fin.at[1, slot], sem, to(k))

        each(0, 4, one)

        @pl.when(flag)
        def _():
            fin[1, slot] = fin[0, quarter]

    def wait_last(fin, flag, sem):
        @pl.when(flag)
        def _():
            drain(fin.at[0, pl.ds(0, 3)], sem)

        @pl.when(jnp.logical_not(flag))
        def _():
            drain(fin.at[0], sem)

    arrive(26)
    last(jnp.sum(sum_i[0:8].astype(F32), axis=0), fin_i, self_i, (y % 2) * 2 + x % 2, to_i, 28)
    arrive(24)
    last(jnp.sum(sum_t[...].astype(F32), axis=0), fin_t, self_t, (z // 4) * 2 + z % 2, to_t, 27)

    def finish(o_ref, fin, flag, sem):
        wait_last(fin, flag, rsem.at[sem])
        for k in range(2):
            o_ref[:, 128 * k:128 * k + 128] = fin[1, k, 0:20, :] + fin[1, 2 + k, 0:20, :]

    finish(oi_ref, fin_i, self_i, 28)
    finish(ot_ref, fin_t, self_t, 27)

    for i, ref in sent.items():
        drain(ref, ssem.at[i])
    wait_last(fin_t, self_t, ssem.at[27])
    wait_last(fin_i, self_i, ssem.at[28])


def per_device(feat_img, feat_txt, w_img, w_txt, logit_scale):
    v = pl.BlockSpec(memory_space=pltpu.VMEM)
    out = jax.ShapeDtypeStruct((20, 256), F32)
    vm = pltpu.VMEM
    return pl.pallas_call(
        kernel,
        out_shape=(out, out),
        in_specs=[pl.BlockSpec(memory_space=pltpu.SMEM)] + [pl.BlockSpec(memory_space=pl.ANY)] * 4,
        out_specs=(v, v),
        scratch_shapes=[
            vm((2, 2, 32, 1280), BF16), vm((2, 2, 32, 1280), BF16), vm((1280, 256), BF16), vm((1280, 256), BF16),
            vm((2, 4, 32, 256), F32), vm((2, 4, 32, 256), F32),
            vm((512, 1024), BF16), vm((512, 1024), BF16),
            vm((4, 2, 32, 1280), BF16), vm((2, 4, 32, 1280), BF16),
            vm((1024, 512), BF16), vm((1024, 512), BF16),
            vm((1280, 256), BF16), vm((1280, 256), BF16),
            vm((16, 8, 128), F32), vm((16, 8, 128), F32),
            vm((512, 512), F32), vm((512, 512), F32),
            vm((4, 4, 2, 64, 256), F32),
            vm((4, 4, 64, 256), BF16), vm((4, 4, 64, 256), BF16), vm((4, 4, 64, 256), BF16), vm((4, 4, 64, 256), BF16),
            vm((4, 64, 256), BF16), vm((4, 64, 256), BF16), vm((4, 64, 256), BF16), vm((4, 64, 256), BF16),
            vm((8, 128, 256), F32), vm((2, 4, 128, 256), BF16), vm((2, 4, 128, 256), BF16),
            vm((8, 128, 256), BF16), vm((2, 128, 256), BF16), vm((2, 64, 256), BF16), vm((2, 128, 256), BF16),
            vm((4, 128, 256), BF16),
            vm((16, 80, 128), F32), vm((16, 80, 128), BF16),
            vm((16, 80, 128), BF16), vm((16, 80, 128), BF16),
            vm((8, 80, 128), F32), vm((8, 80, 128), F32),
            vm((2, 4, 24, 128), F32), vm((2, 4, 24, 128), F32),
            pltpu.SemaphoreType.DMA((34,)), pltpu.SemaphoreType.DMA((34,)), pltpu.SemaphoreType.DMA((4,)),
        ],
        compiler_params=pltpu.CompilerParams(
            collective_id=0, has_side_effects=True, vmem_limit_bytes=56 * 2 ** 20),
        name="contrastive",
    )(logit_scale.reshape(1, 1), feat_img.reshape(2, 2, 32, 1280), feat_txt.reshape(2, 2, 32, 1280), w_img, w_txt)


def solution(mesh):
    return jax.shard_map(
        per_device,
        mesh=mesh,
        in_specs=(P("dp", None), P("dp", None), P(None, "head"), P(None, "head"), P()),
        out_specs=(P("dp", "head"), P("dp", "head")),
        check_vma=False,
    )
```

```python
import jax
import jax.numpy as jnp
from jax import lax
from jax.experimental import pallas as pl
from jax.experimental.pallas import tpu as pltpu
from jax.sharding import PartitionSpec as P

MESH = pl.DeviceIdType.MESH
F32 = jnp.float32
BF16 = jnp.bfloat16
NT = (((1,), (1,)), ((), ()))
NN = (((1,), (0,)), ((), ()))


def device(x, y, z, core):
    x, y, z = (x + 4) % 4, (y + 4) % 4, (z + 8) % 8
    return {"dp": (x * 8 + z) * 2 + y % 2, "head": (y // 2) * 2 + core}


def place():
    d = lax.axis_index("dp")
    h = lax.axis_index("head")
    return d // 16, (h // 2) * 2 + d % 2, (d // 2) % 8, h % 2


def image_slot(x, y):
    x, y = (x + 4) % 4, (y + 4) % 4
    return (y % 2) * 8 + x * 2 + y // 2


def text_slot(z, core):
    z = (z + 8) % 8
    return (z // 4) * 8 + core * 4 + z % 4


def rows(slot, count=32, shift=0):
    return pl.ds(pl.multiple_of(slot * 32 + shift, 16), count)


def drain(ref, sem):
    pltpu.make_async_copy(ref, ref, sem).wait()


def each(steps, body):
    for k in steps:
        body(k)


def hops(k, n):
    return min(k % n, n - k % n)


PLANE = sorted(range(1, 16), key=lambda k: -hops(k, 4) - hops(k // 4, 4))
LINE = sorted(range(1, 16), key=lambda k: -hops(k, 8))
COLUMN = [k for k in LINE if k < 8]


def to_column(row):
    eye = lax.broadcasted_iota(jnp.int32, (128, 128), 0) == lax.broadcasted_iota(jnp.int32, (128, 128), 1)
    return jnp.concatenate(
        [jnp.sum(jnp.where(eye, row[:, 128 * k:128 * k + 128], 0.0), axis=1, keepdims=True)
         for k in range(row.shape[1] // 128)], axis=0)


def lse_rows(a):
    top = jnp.max(a, axis=0, keepdims=True)
    return top + jnp.log(jnp.sum(jnp.exp(a - top), axis=0, keepdims=True))


def put_stats(ref, lse, inv):
    for k in range(4):
        ref[k:k + 1, :] = lse[:, 128 * k:128 * k + 128]
    pick = lax.broadcasted_iota(jnp.int32, (32, 128), 0) == lax.broadcasted_iota(jnp.int32, (32, 128), 1)
    ref[4:5, :] = jnp.sum(jnp.where(pick, inv, 0.0), axis=0, keepdims=True)


def merged_stats(ref):
    a = ref[:, 0:4, :]
    top = jnp.max(a, axis=0)
    lse = top + jnp.log(jnp.sum(jnp.exp(a - top[None]), axis=0))
    lse = jnp.concatenate([lse[k:k + 1, :] for k in range(4)], axis=1)
    inv = jnp.concatenate([ref[k, 4:5, 0:32] for k in range(16)], axis=1)
    return lse, inv


def kernel(scale_ref, fi_ref, ft_ref, wi_ref, wt_ref, o_ref,
           fi_v, ft_v, wi_v, wt_v,
           raw_s, raw_r, emb_i, emb_t, feat_i, feat_t, emb_it, emb_tt, feat_it, feat_tt,
           stat_i, stat_t, log_a, log_b, own_i, dem_x, dem_y, get_x, get_y, dem_x2, dem_y2, last_x, last_y,
           own_t, dem_t, sib_r, sib_s, full_z, half_z, sum_z, get_t,
           par_i, par_t, sum_i, sum_t, out_s, out_r, fin_i, fin_t, ssem, rsem, lsem):
    x, y, z, core = place()
    h = lax.axis_index("head")
    slot_i = image_slot(x, y)
    slot_t = text_slot(z, core)
    sibling = device(x, y, z, 1 - core)
    due = {}
    sent = {}

    def send(src, dst, sem, peer, arrival=None):
        pltpu.make_async_remote_copy(
            src_ref=src, dst_ref=dst, send_sem=ssem.at[sem], recv_sem=rsem.at[sem if arrival is None else arrival],
            device_id=peer, device_id_type=MESH,
        ).start()

    def arrive(i):
        drain(due.pop(i), rsem.at[i])

    def head_peer(k):
        return {"dp": lax.axis_index("dp"), "head": (h + k) % 4}

    def plane_peer(k):
        return device(x + k % 4, y + k // 4, z, core)

    def line_peer(k):
        return device(x, y, z + k % 8, (core + k // 8) % 2)

    self_i = (z % 2 == x // 2) & (core == x % 2) & (core == x // 2)
    self_t = (y == z // 2) & (core == y // 2) & ((z % 4) // 2 == core)
    quarter = (z % 2) * 2 + y % 2

    def to_i(e):
        return device((z % 2) * 2 + core, (y // 2) * 2 + e % 2, (z // 2) * 2 + e // 2, x // 2)

    def to_t(e):
        return device(x, core * 2 + e % 2, 2 * y + e // 2, (z % 4) // 2)

    bar = pltpu.get_barrier_semaphore()

    def hello(peer):
        pl.semaphore_signal(bar, inc=1, device_id=peer, device_id_type=MESH)

    each(range(1, 4), lambda k: hello(head_peer(k)))
    each(range(1, 4), lambda k: hello(device(x + k, y, z, core)))
    hello(device(x, y + 1, z, core))
    hello(device(x, y - 1, z, core))
    each(range(1, 4), lambda k: hello(device(x, y, z + k, core)))
    each(range(1, 4), lambda k: hello(device(x, y, z - k, core)))

    fetched = [pltpu.make_async_copy(a, b, lsem.at[k])
               for k, (a, b) in enumerate(((fi_ref, fi_v), (wi_ref, wi_v), (ft_ref, ft_v), (wt_ref, wt_v)))]
    for copy in fetched:
        copy.start()

    for side, (f, w) in enumerate(((fi_v, wi_v), (ft_v, wt_v))):
        fetched[2 * side].wait()
        fetched[2 * side + 1].wait()
        raw = jnp.dot(f[...].reshape(128, 1280), w[...], preferred_element_type=F32)
        raw_s[side] = raw.reshape(4, 32, 256)

    pl.semaphore_wait(bar, 14)

    def send_raw(side, sem):
        def one(k):
            peer = head_peer(k)
            send(raw_s.at[side, peer["head"]], raw_r.at[side, h], sem, peer)
        each(range(1, 4), one)
        due[sem] = sent[sem] = raw_s.at[side, pl.ds(0, 3)]
        raw_r[side, h] = raw_s[side, h]

    send_raw(0, 0)
    send_raw(1, 1)

    def unit_rows(side):
        whole = jnp.concatenate([raw_r[side, k] for k in range(4)], axis=1)
        inv = lax.rsqrt(jnp.sum(whole * whole, axis=1, keepdims=True) + 1e-06)
        return (whole * inv).astype(BF16), inv

    order = (1, 3, 2)
    mine_i = rows(slot_i)
    mine_t = rows(slot_t)
    arrive(0)
    unit_i, inv_i = unit_rows(0)
    emb_i[mine_i, :] = unit_i
    for k in order:
        send(emb_i.at[mine_i], emb_i.at[mine_i], 4, device(x + k, y, z, core), 4 + k)
        send(emb_i.at[mine_i], emb_i.at[mine_i], 4, device(x, y + k, z, core), 7 + k)
        due[4 + k] = due[7 + k] = emb_i.at[rows(0)]
    arrive(1)
    unit_t, inv_t = unit_rows(1)
    emb_t[mine_t, :] = unit_t
    for k, s in enumerate((2, -2, 1, -1)):
        send(emb_t.at[mine_t], emb_t.at[mine_t], 12, device(x, y, z + s, core), 12 + k)
        due[12 + k] = emb_t.at[rows(0)]

    def forward_x(k):
        arrive(4 + k)
        block = rows(image_slot(x - k, y), 16)
        for j in order:
            send(emb_i.at[block], emb_i.at[block], 4, device(x, y + j, z, core), 11)

    def forward_y(k):
        arrive(7 + k)
        block = rows(image_slot(x, y - k), 16, 16)
        for j in order:
            send(emb_i.at[block], emb_i.at[block], 4, device(x + j, y, z, core), 11)

    def forward_z(k, s):
        arrive(12 + k)
        block = rows(text_slot(z + 2 * s, core))
        send(emb_t.at[block], emb_t.at[block], 12, device(x, y, z - s, core), 16)
        block = rows(text_slot(z + 2 * s, core), 16, 16 * k)
        send(emb_t.at[block], emb_t.at[block], 12, device(x, y, z - 2 * s, core), 16)

    def to_sibling(z_from):
        block = rows(text_slot(z_from, core))
        send(emb_t.at[block], emb_t.at[block], 17, sibling)

    to_sibling(z)
    forward_x(1)
    forward_y(1)
    forward_x(3)
    forward_y(3)
    forward_z(0, -1)
    forward_z(1, 1)
    forward_x(2)
    forward_y(2)
    due[11] = emb_i.at[rows(0, 288)]
    due[16] = emb_t.at[rows(0, 96)]
    sent[4] = emb_i.at[rows(0, 480)]
    sent[12] = emb_t.at[rows(0, 224)]
    to_sibling(z - 2)
    to_sibling(z + 2)
    arrive(14)
    to_sibling(z - 1)
    arrive(15)
    to_sibling(z + 1)
    arrive(16)
    to_sibling(z + 3)
    to_sibling(z - 3)
    to_sibling(z + 4)
    due[17] = sent[17] = emb_t.at[pl.ds(0, 256)]
    arrive(11)

    scale = scale_ref[0, 0]

    def logits(part):
        where = [pl.ds(pl.multiple_of(256 * k + 128 * part, 128), 128) for k in range(2)]
        texts = jnp.concatenate([emb_t[r, :] for r in where], axis=0)
        a = scale * lax.dot_general(texts, emb_i[...], NT, preferred_element_type=F32)
        for k in range(2):
            log_b[where[k], :] = a[128 * k:128 * k + 128]

    logits(core)
    arrive(17)
    logits(1 - core)
    put_stats(stat_i.at[slot_i], lse_rows(log_b[...]), inv_i)
    each(PLANE, lambda k: send(stat_i.at[slot_i], stat_i.at[slot_i], 18, plane_peer(k)))
    due[18] = sent[18] = stat_i.at[pl.ds(0, 15)]
    log_a[...] = log_b[...].T
    put_stats(stat_t.at[slot_t], lse_rows(log_a[...]), inv_t)
    each(LINE, lambda k: send(stat_t.at[slot_t], stat_t.at[slot_t], 19, line_peer(k)))
    due[19] = sent[19] = stat_t.at[pl.ds(0, 15)]
    each(range(1, 4), lambda k: send(fi_v.at[:, core], feat_i.at[x], 2, device(x + k, y, z, core)))
    due[2] = sent[2] = feat_i.at[pl.ds(0, 3)]
    feat_i[x] = fi_v[:, core]
    each(range(1, 4), lambda k: send(ft_v.at[y // 2, core], feat_t.at[core, z % 4], 3,
                              device(x, y, (z // 4) * 4 + (z + k) % 4, core)))
    due[3] = sent[3] = feat_t.at[0, pl.ds(0, 3)]
    feat_t[core, z % 4] = ft_v[y // 2, core]

    emb_it[...] = emb_i[...].T
    emb_tt[...] = emb_t[...].T
    arrive(18)
    arrive(19)
    row_lse, invs_i = merged_stats(stat_i)
    col_lse, invs_t = merged_stats(stat_t)

    factor = 1.0 / (2.0 * (64.0 * 2.0 ** 0.5))
    ids0 = lax.broadcasted_iota(jnp.int32, (512, 512), 0)
    ids1 = lax.broadcasted_iota(jnp.int32, (512, 512), 1)

    a = log_a[...]
    same = (ids0 // 32 == slot_i) & (ids0 - ids1 == 32 * (slot_i - slot_t))
    g = (jnp.exp(a - to_column(row_lse)) + jnp.exp(a - col_lse) - jnp.where(same, 2.0, 0.0)) * factor
    g = g.astype(BF16)
    inner_t = jnp.sum(g.astype(F32) * a, axis=0, keepdims=True)

    def demb(g, inner, base, unit, half):
        part = pl.ds(pl.multiple_of(512 * half, 512), 512)
        d = scale * lax.dot_general(base[part, :], g, NN, preferred_element_type=F32)
        return d - unit[part, :].astype(F32) * inner

    d = demb(g, inner_t, emb_it, emb_tt, 1 - core)
    for k in range(2):
        dem_t[k] = d[:, 256 * k:256 * k + 256].astype(BF16).reshape(4, 128, 256)
    send(dem_t, sib_r, 21, sibling)
    due[21] = sent[21] = sib_r
    gt = g.T
    inner_i = jnp.sum(gt.astype(F32) * log_b[...], axis=0, keepdims=True)

    def image_half(pair):
        d = demb(gt, inner_i, emb_tt, emb_it, pair)
        for k in range(2):
            py = 2 * pair + k
            e = d[:, 256 * k:256 * k + 256].reshape(4, 2, 64, 256)
            own_i[py] = e
            dem_x[:, py] = e[:, 0].astype(BF16)
            dem_y[py] = e[:, 1].astype(BF16)

    def send_y(py):
        send(dem_y.at[py], get_y.at[y], 29, device(x, py, z, core))

    image_half(1 - y // 2)
    send_y((y + 2) % 4)
    send_y((1 - y // 2) * 2 + (y + 1) % 2)
    image_half(y // 2)
    each(range(0, 3), lambda k: send(dem_x.at[(x + 1 + (k + 1) % 3) % 4], get_x.at[x], 22, device(x + 1 + (k + 1) % 3, y, z, core)))
    send_y((y // 2) * 2 + (y + 1) % 2)
    due[22] = sent[22] = get_x.at[pl.ds(0, 3)]
    due[29] = sent[29] = get_y.at[pl.ds(0, 3)]
    d = demb(g, inner_t, emb_it, emb_tt, core)
    for k in range(2):
        own_t[4 * k:4 * k + 4] = d[:, 256 * k:256 * k + 256].reshape(4, 128, 256)

    arrive(21)
    own_t[...] = own_t[...] + sib_r[...].astype(F32).reshape(8, 128, 256)
    sib_s[...] = own_t[...].astype(BF16)
    for k, s in enumerate((1, -1)):
        far = (z + 4) % 8
        half = pl.ds(64 * k, 64)
        send(sib_s.at[far, half], half_z.at[k], 30, device(x, y, z + 2 * s, core))
        send(sib_s.at[(z + 3 * s + 8) % 8], full_z.at[k], 23, device(x, y, z + s, core))
        send(sib_s.at[(z + s + 8) % 8], get_t.at[k], 31, device(x, y, z + s, core))
    due[23] = sent[23] = full_z
    due[30] = sent[30] = half_z

    arrive(3)
    send(feat_t.at[core], feat_t.at[core], 20, sibling)
    due[20] = sent[20] = feat_t.at[0]
    arrive(2)
    feat_it[...] = feat_i[...].reshape(256, 1280).T
    arrive(20)
    feat_tt[...] = feat_t[...].reshape(256, 1280).T

    arrive(29)
    for k in range(1, 4):
        px = (x + k) % 4
        total = own_i[y, px, 1]
        for j in range(1, 4):
            total += get_y[(y + j) % 4, px].astype(F32)
        dem_y2[px] = total.astype(BF16)
        send(dem_y2.at[px], last_y.at[x], 32, device(px, y, z, core))
    due[32] = sent[32] = last_y.at[pl.ds(0, 3)]
    arrive(22)
    for k in range(1, 4):
        py = (y + k) % 4
        total = own_i[py, x, 0]
        for j in range(1, 4):
            total += get_x[(x + j) % 4, py].astype(F32)
        dem_x2[py] = total.astype(BF16)
        send(dem_x2.at[py], last_x.at[y], 33, device(x, py, z, core))
    due[33] = sent[33] = last_x.at[pl.ds(0, 3)]
    arrive(23)
    arrive(30)
    for k, s in enumerate((1, -1)):
        dest = (z + 2 * s + 8) % 8
        total = own_t[dest] + full_z[k].astype(F32)
        extra = half_z[k].astype(F32)
        blank = jnp.zeros_like(extra)
        total += jnp.concatenate([extra, blank] if k == 0 else [blank, extra], axis=0)
        sum_z[k] = total.astype(BF16)
        send(sum_z.at[k], get_t.at[2 + k], 31, device(x, y, z + 2 * s, core))
    due[31] = sent[31] = get_t

    def weights(total, invs, upper, feats):
        inv = jnp.where(upper, invs[:, 256:512], invs[:, 0:256])
        draw = inv * total
        high = draw.astype(BF16)
        low = (draw - high.astype(F32)).astype(BF16)
        f = feats[...]
        out = lax.dot_general(f, high, NT, preferred_element_type=F32)
        out += lax.dot_general(f, low, NT, preferred_element_type=F32)
        return out.reshape(16, 80, 128)

    def image_sum(own, first, lines, last, at):
        total = own
        for j in range(1, 4):
            total += first((at + j) % 4).astype(F32)
            total += last[(lines + j) % 4].astype(F32)
        return total

    arrive(32)
    arrive(33)
    def chunk_i(pz, pc):
        return ((pz % 2) * 2 + pc) * 4 + pz // 2

    upper_cols = image_sum(own_i[y, x, 0], lambda j: get_x[j, y], y, last_x, x)
    lower_cols = image_sum(own_i[y, x, 1], lambda j: get_y[j, x], x, last_y, y)
    total_i = jnp.concatenate([upper_cols, lower_cols], axis=0)
    par_i[...] = weights(total_i, invs_i, y % 2 == 1, feat_it)
    for k in range(8):
        out_s[k] = par_i[chunk_i(k, 1 - core)]
    send(out_s, out_r, 25, sibling)
    due[25] = sent[25] = out_r
    arrive(31)
    total_t = own_t[z] + jnp.sum(get_t[...].astype(F32), axis=0)
    par_t[...] = weights(total_t, invs_t, z // 4 == 1, feat_tt).astype(BF16)

    def part_t(k):
        px, py = (x + k % 4) % 4, (y + k // 4) % 4
        send(par_t.at[px * 4 + py], sum_t.at[slot_i], 24, plane_peer(k))

    each(PLANE, part_t)
    due[24] = sent[24] = sum_t.at[pl.ds(0, 15)]
    sum_t[slot_i] = par_t[x * 4 + y]

    arrive(25)
    for k in range(8):
        par_t_i = par_i[chunk_i(k, core)] + out_r[k]
        sib_p = par_t_i.astype(BF16)
        sum_i[8 + k] = sib_p

    def part_i(k):
        send(sum_i.at[8 + (z + k) % 8], sum_i.at[z], 26, line_peer(k))

    each(COLUMN, part_i)
    due[26] = sent[26] = sum_i.at[pl.ds(0, 7)]
    sum_i[z] = sum_i[8 + z]

    def last(total, fin, flag, slot, to, sem):
        for k in range(4):
            fin[0, k, 0:20, :] = total[20 * k:20 * k + 20, :]

        def one(k):
            @pl.when(jnp.logical_not(flag & (k == quarter)))
            def _():
                send(fin.at[0, k], fin.at[1, slot], sem, to(k))

        each(range(0, 4), one)

        @pl.when(flag)
        def _():
            fin[1, slot] = fin[0, quarter]

    def wait_last(fin, flag, sem):
        @pl.when(flag)
        def _():
            drain(fin.at[0, pl.ds(0, 3)], sem)

        @pl.when(jnp.logical_not(flag))
        def _():
            drain(fin.at[0], sem)

    arrive(26)
    last(jnp.sum(sum_i[0:8].astype(F32), axis=0), fin_i, self_i, (y % 2) * 2 + x % 2, to_i, 28)
    arrive(24)
    last(jnp.sum(sum_t[...].astype(F32), axis=0), fin_t, self_t, (z // 4) * 2 + z % 2, to_t, 27)

    def finish(o_ref, fin, flag, sem):
        wait_last(fin, flag, rsem.at[sem])
        for k in range(2):
            o_ref[:, 128 * k:128 * k + 128] = fin[1, k, 0:20, :] + fin[1, 2 + k, 0:20, :]

    finish(o_ref.at[0], fin_i, self_i, 28)
    finish(o_ref.at[1], fin_t, self_t, 27)

    for i, ref in sent.items():
        drain(ref, ssem.at[i])
    wait_last(fin_t, self_t, ssem.at[27])
    wait_last(fin_i, self_i, ssem.at[28])


def per_device(feat_img, feat_txt, w_img, w_txt, logit_scale):
    v = pl.BlockSpec(memory_space=pltpu.VMEM)
    out = jax.ShapeDtypeStruct((2, 20, 256), F32)
    vm = pltpu.VMEM
    o = pl.pallas_call(
        kernel,
        out_shape=out,
        in_specs=[pl.BlockSpec(memory_space=pltpu.SMEM)] + [pl.BlockSpec(memory_space=pl.ANY)] * 4,
        out_specs=v,
        scratch_shapes=[
            vm((2, 2, 32, 1280), BF16), vm((2, 2, 32, 1280), BF16), vm((1280, 256), BF16), vm((1280, 256), BF16),
            vm((2, 4, 32, 256), F32), vm((2, 4, 32, 256), F32),
            vm((512, 1024), BF16), vm((512, 1024), BF16),
            vm((4, 2, 32, 1280), BF16), vm((2, 4, 32, 1280), BF16),
            vm((1024, 512), BF16), vm((1024, 512), BF16),
            vm((1280, 256), BF16), vm((1280, 256), BF16),
            vm((16, 8, 128), F32), vm((16, 8, 128), F32),
            vm((512, 512), F32), vm((512, 512), F32),
            vm((4, 4, 2, 64, 256), F32),
            vm((4, 4, 64, 256), BF16), vm((4, 4, 64, 256), BF16), vm((4, 4, 64, 256), BF16), vm((4, 4, 64, 256), BF16),
            vm((4, 64, 256), BF16), vm((4, 64, 256), BF16), vm((4, 64, 256), BF16), vm((4, 64, 256), BF16),
            vm((8, 128, 256), F32), vm((2, 4, 128, 256), BF16), vm((2, 4, 128, 256), BF16),
            vm((8, 128, 256), BF16), vm((2, 128, 256), BF16), vm((2, 64, 256), BF16), vm((2, 128, 256), BF16),
            vm((4, 128, 256), BF16),
            vm((16, 80, 128), F32), vm((16, 80, 128), BF16),
            vm((16, 80, 128), BF16), vm((16, 80, 128), BF16),
            vm((8, 80, 128), F32), vm((8, 80, 128), F32),
            vm((2, 4, 24, 128), F32), vm((2, 4, 24, 128), F32),
            pltpu.SemaphoreType.DMA((34,)), pltpu.SemaphoreType.DMA((34,)), pltpu.SemaphoreType.DMA((4,)),
        ],
        compiler_params=pltpu.CompilerParams(
            collective_id=0, has_side_effects=True, vmem_limit_bytes=56 * 2 ** 20),
        name="contrastive",
    )(logit_scale.reshape(1, 1), feat_img.reshape(2, 2, 32, 1280), feat_txt.reshape(2, 2, 32, 1280), w_img, w_txt)
    return o[0], o[1]


def solution(mesh):
    return jax.shard_map(
        per_device,
        mesh=mesh,
        in_specs=(P("dp", None), P("dp", None), P(None, "head"), P(None, "head"), P()),
        out_specs=(P("dp", "head"), P("dp", "head")),
        check_vma=False,
    )
```

```python
import jax
import jax.numpy as jnp
from jax import lax
from jax.experimental import pallas as pl
from jax.experimental.pallas import tpu as pltpu
from jax.sharding import PartitionSpec as P

MESH = pl.DeviceIdType.MESH
F32 = jnp.float32
BF16 = jnp.bfloat16
NT = (((1,), (1,)), ((), ()))
NN = (((1,), (0,)), ((), ()))


def device(x, y, z, core):
    x, y, z = (x + 4) % 4, (y + 4) % 4, (z + 8) % 8
    return {"dp": (x * 8 + z) * 2 + y % 2, "head": (y // 2) * 2 + core}


def place():
    d = lax.axis_index("dp")
    h = lax.axis_index("head")
    return d // 16, (h // 2) * 2 + d % 2, (d // 2) % 8, h % 2


def image_slot(x, y):
    x, y = (x + 4) % 4, (y + 4) % 4
    return (y % 2) * 8 + x * 2 + y // 2


def text_slot(z, core):
    z = (z + 8) % 8
    return (z // 4) * 8 + core * 4 + z % 4


def rows(slot, count=32, shift=0):
    return pl.ds(pl.multiple_of(slot * 32 + shift, 16), count)


def drain(ref, sem):
    pltpu.make_async_copy(ref, ref, sem).wait()


def each(steps, body):
    for k in steps:
        body(k)


def hops(k, n):
    return min(k % n, n - k % n)


PLANE = sorted(range(1, 16), key=lambda k: -hops(k, 4) - hops(k // 4, 4))
LINE = sorted(range(1, 16), key=lambda k: -hops(k, 8))
COLUMN = [k for k in LINE if k < 8]


def to_column(row):
    eye = lax.broadcasted_iota(jnp.int32, (128, 128), 0) == lax.broadcasted_iota(jnp.int32, (128, 128), 1)
    return jnp.concatenate(
        [jnp.sum(jnp.where(eye, row[:, 128 * k:128 * k + 128], 0.0), axis=1, keepdims=True)
         for k in range(row.shape[1] // 128)], axis=0)


def lse_rows(a):
    top = jnp.max(a, axis=0, keepdims=True)
    return top + jnp.log(jnp.sum(jnp.exp(a - top), axis=0, keepdims=True))


def put_stats(ref, lse, inv):
    for k in range(4):
        ref[k:k + 1, :] = lse[:, 128 * k:128 * k + 128]
    pick = lax.broadcasted_iota(jnp.int32, (32, 128), 0) == lax.broadcasted_iota(jnp.int32, (32, 128), 1)
    ref[4:5, :] = jnp.sum(jnp.where(pick, inv, 0.0), axis=0, keepdims=True)


def merged_stats(ref):
    a = ref[:, 0:4, :]
    top = jnp.max(a, axis=0)
    lse = top + jnp.log(jnp.sum(jnp.exp(a - top[None]), axis=0))
    lse = jnp.concatenate([lse[k:k + 1, :] for k in range(4)], axis=1)
    inv = jnp.concatenate([ref[k, 4:5, 0:32] for k in range(16)], axis=1)
    return lse, inv


def kernel(scale_ref, fi_ref, ft_ref, wi_ref, wt_ref, o_ref,
           fi_v, ft_v, wi_v, wt_v,
           raw_s, raw_r, emb_i, emb_t, feat_i, feat_t, emb_it, emb_tt, feat_it, feat_tt,
           stat_i, stat_t, log_a, log_b, own_i, dem_x, dem_y, get_x, get_y, dem_x2, dem_y2, last_x, last_y,
           own_t, dem_t, sib_r, sib_s, full_z, half_z, sum_z, get_t,
           par_i, par_t, line_s, sum_i, sum_t, out_s, out_r, fin_i, fin_t, ssem, rsem, lsem):
    x, y, z, core = place()
    h = lax.axis_index("head")
    slot_i = image_slot(x, y)
    slot_t = text_slot(z, core)
    sibling = device(x, y, z, 1 - core)
    due = {}
    sent = {}

    def send(src, dst, sem, peer, arrival=None):
        pltpu.make_async_remote_copy(
            src_ref=src, dst_ref=dst, send_sem=ssem.at[sem], recv_sem=rsem.at[sem if arrival is None else arrival],
            device_id=peer, device_id_type=MESH,
        ).start()

    def arrive(i):
        drain(due.pop(i), rsem.at[i])

    def head_peer(k):
        return {"dp": lax.axis_index("dp"), "head": (h + k) % 4}

    def plane_peer(k):
        return device(x + k % 4, y + k // 4, z, core)

    def line_peer(k):
        return device(x, y, z + k % 8, (core + k // 8) % 2)

    self_i = (z % 2 == x // 2) & (core == x % 2) & (core == x // 2)
    quarter = (z % 2) * 2 + y % 2

    def to_i(e):
        return device((z % 2) * 2 + core, (y // 2) * 2 + e % 2, (z // 2) * 2 + e // 2, x // 2)

    def text_pair(py):
        step = 1 - 2 * (z % 2)
        inside = jnp.where(py % 2 == 0, 2, step)
        outside = jnp.where(py % 2 == 0, -step, 0)
        return (z // 2 + jnp.where(py // 2 == core, inside, outside) + 4) % 4

    def to_t(e):
        return device(x, core * 2 + e % 2, 2 * text_pair(y) + e // 2, (z % 4) // 2)

    bar = pltpu.get_barrier_semaphore()

    def hello(peer):
        pl.semaphore_signal(bar, inc=1, device_id=peer, device_id_type=MESH)

    each(range(1, 4), lambda k: hello(head_peer(k)))
    each(range(1, 4), lambda k: hello(device(x + k, y, z, core)))
    hello(device(x, y + 1, z, core))
    hello(device(x, y - 1, z, core))
    each(range(1, 4), lambda k: hello(device(x, y, z + k, core)))
    each(range(1, 4), lambda k: hello(device(x, y, z - k, core)))

    fetched = [pltpu.make_async_copy(a, b, lsem.at[k])
               for k, (a, b) in enumerate(((fi_ref, fi_v), (wi_ref, wi_v), (ft_ref, ft_v), (wt_ref, wt_v)))]
    for copy in fetched:
        copy.start()

    for side, (f, w) in enumerate(((fi_v, wi_v), (ft_v, wt_v))):
        fetched[2 * side].wait()
        fetched[2 * side + 1].wait()
        raw = jnp.dot(f[...].reshape(128, 1280), w[...], preferred_element_type=F32)
        raw_s[side] = raw.reshape(4, 32, 256)

    pl.semaphore_wait(bar, 14)

    def send_raw(side, sem):
        def one(k):
            peer = head_peer(k)
            send(raw_s.at[side, peer["head"]], raw_r.at[side, h], sem, peer)
        each(range(1, 4), one)
        due[sem] = sent[sem] = raw_s.at[side, pl.ds(0, 3)]
        raw_r[side, h] = raw_s[side, h]

    send_raw(0, 0)
    send_raw(1, 1)

    def unit_rows(side):
        whole = jnp.concatenate([raw_r[side, k] for k in range(4)], axis=1)
        inv = lax.rsqrt(jnp.sum(whole * whole, axis=1, keepdims=True) + 1e-06)
        return (whole * inv).astype(BF16), inv

    order = (1, 3, 2)
    mine_i = rows(slot_i)
    mine_t = rows(slot_t)
    arrive(0)
    unit_i, inv_i = unit_rows(0)
    emb_i[mine_i, :] = unit_i
    for k in order:
        send(emb_i.at[mine_i], emb_i.at[mine_i], 4, device(x + k, y, z, core), 4 + k)
        send(emb_i.at[mine_i], emb_i.at[mine_i], 4, device(x, y + k, z, core), 7 + k)
        due[4 + k] = due[7 + k] = emb_i.at[rows(0)]
    arrive(1)
    unit_t, inv_t = unit_rows(1)
    emb_t[mine_t, :] = unit_t
    for k, s in enumerate((2, -2, 1, -1)):
        send(emb_t.at[mine_t], emb_t.at[mine_t], 12, device(x, y, z + s, core), 12 + k)
        due[12 + k] = emb_t.at[rows(0)]

    def forward_x(k):
        arrive(4 + k)
        block = rows(image_slot(x - k, y), 16)
        for j in order:
            send(emb_i.at[block], emb_i.at[block], 4, device(x, y + j, z, core), 11)

    def forward_y(k):
        arrive(7 + k)
        block = rows(image_slot(x, y - k), 16, 16)
        for j in order:
            send(emb_i.at[block], emb_i.at[block], 4, device(x + j, y, z, core), 11)

    def forward_z(k, s):
        arrive(12 + k)
        block = rows(text_slot(z + 2 * s, core))
        send(emb_t.at[block], emb_t.at[block], 12, device(x, y, z - s, core), 16)
        block = rows(text_slot(z + 2 * s, core), 16, 16 * k)
        send(emb_t.at[block], emb_t.at[block], 12, device(x, y, z - 2 * s, core), 16)

    def to_sibling(z_from):
        block = rows(text_slot(z_from, core))
        send(emb_t.at[block], emb_t.at[block], 17, sibling)

    to_sibling(z)
    forward_x(1)
    forward_y(1)
    forward_x(3)
    forward_y(3)
    forward_z(0, -1)
    forward_z(1, 1)
    forward_x(2)
    forward_y(2)
    due[11] = emb_i.at[rows(0, 288)]
    due[16] = emb_t.at[rows(0, 96)]
    sent[4] = emb_i.at[rows(0, 480)]
    sent[12] = emb_t.at[rows(0, 224)]
    to_sibling(z - 2)
    to_sibling(z + 2)
    arrive(14)
    to_sibling(z - 1)
    arrive(15)
    to_sibling(z + 1)
    arrive(16)
    to_sibling(z + 3)
    to_sibling(z - 3)
    to_sibling(z + 4)
    due[17] = sent[17] = emb_t.at[pl.ds(0, 256)]
    arrive(11)

    scale = scale_ref[0, 0]

    def logits(part):
        where = [pl.ds(pl.multiple_of(256 * k + 128 * part, 128), 128) for k in range(2)]
        texts = jnp.concatenate([emb_t[r, :] for r in where], axis=0)
        a = scale * lax.dot_general(texts, emb_i[...], NT, preferred_element_type=F32)
        for k in range(2):
            log_b[where[k], :] = a[128 * k:128 * k + 128]

    logits(core)
    arrive(17)
    logits(1 - core)
    put_stats(stat_i.at[slot_i], lse_rows(log_b[...]), inv_i)
    each(PLANE, lambda k: send(stat_i.at[slot_i], stat_i.at[slot_i], 18, plane_peer(k)))
    due[18] = sent[18] = stat_i.at[pl.ds(0, 15)]
    log_a[...] = log_b[...].T
    put_stats(stat_t.at[slot_t], lse_rows(log_a[...]), inv_t)
    each(LINE, lambda k: send(stat_t.at[slot_t], stat_t.at[slot_t], 19, line_peer(k)))
    due[19] = sent[19] = stat_t.at[pl.ds(0, 15)]
    each(range(1, 4), lambda k: send(fi_v.at[:, core], feat_i.at[x], 2, device(x + k, y, z, core)))
    due[2] = sent[2] = feat_i.at[pl.ds(0, 3)]
    feat_i[x] = fi_v[:, core]
    each(range(1, 4), lambda k: send(ft_v.at[y // 2, core], feat_t.at[core, z % 4], 3,
                              device(x, y, (z // 4) * 4 + (z + k) % 4, core)))
    due[3] = sent[3] = feat_t.at[0, pl.ds(0, 3)]
    feat_t[core, z % 4] = ft_v[y // 2, core]

    emb_it[...] = emb_i[...].T
    emb_tt[...] = emb_t[...].T
    arrive(18)
    arrive(19)
    row_lse, invs_i = merged_stats(stat_i)
    col_lse, invs_t = merged_stats(stat_t)

    factor = 1.0 / (2.0 * (64.0 * 2.0 ** 0.5))
    ids0 = lax.broadcasted_iota(jnp.int32, (512, 512), 0)
    ids1 = lax.broadcasted_iota(jnp.int32, (512, 512), 1)

    a = log_a[...]
    same = (ids0 // 32 == slot_i) & (ids0 - ids1 == 32 * (slot_i - slot_t))
    g = (jnp.exp(a - to_column(row_lse)) + jnp.exp(a - col_lse) - jnp.where(same, 2.0, 0.0)) * factor
    g = g.astype(BF16)
    inner_t = jnp.sum(g.astype(F32) * a, axis=0, keepdims=True)

    def demb(g, inner, base, unit, half):
        part = pl.ds(pl.multiple_of(512 * half, 512), 512)
        d = scale * lax.dot_general(base[part, :], g, NN, preferred_element_type=F32)
        return d - unit[part, :].astype(F32) * inner

    d = demb(g, inner_t, emb_it, emb_tt, 1 - core)
    for k in range(2):
        dem_t[k] = d[:, 256 * k:256 * k + 256].astype(BF16).reshape(4, 128, 256)
    send(dem_t, sib_r, 21, sibling)
    due[21] = sent[21] = sib_r
    gt = g.T
    inner_i = jnp.sum(gt.astype(F32) * log_b[...], axis=0, keepdims=True)

    def image_half(pair):
        d = demb(gt, inner_i, emb_tt, emb_it, pair)
        for k in range(2):
            py = 2 * pair + k
            e = d[:, 256 * k:256 * k + 256].reshape(4, 2, 64, 256)
            own_i[py] = e
            dem_x[:, py] = e[:, 0].astype(BF16)
            dem_y[py] = e[:, 1].astype(BF16)

    def send_y(py):
        send(dem_y.at[py], get_y.at[y], 29, device(x, py, z, core))

    image_half(1 - y // 2)
    send_y((y + 2) % 4)
    send_y((1 - y // 2) * 2 + (y + 1) % 2)
    image_half(y // 2)
    each(range(0, 3), lambda k: send(dem_x.at[(x + 1 + (k + 1) % 3) % 4], get_x.at[x], 22, device(x + 1 + (k + 1) % 3, y, z, core)))
    send_y((y // 2) * 2 + (y + 1) % 2)
    due[22] = sent[22] = get_x.at[pl.ds(0, 3)]
    due[29] = sent[29] = get_y.at[pl.ds(0, 3)]
    d = demb(g, inner_t, emb_it, emb_tt, core)
    for k in range(2):
        own_t[4 * k:4 * k + 4] = d[:, 256 * k:256 * k + 256].reshape(4, 128, 256)

    arrive(21)
    own_t[...] = own_t[...] + sib_r[...].astype(F32).reshape(8, 128, 256)
    sib_s[...] = own_t[...].astype(BF16)
    for k, s in enumerate((1, -1)):
        far = (z + 4) % 8
        half = pl.ds(64 * k, 64)
        send(sib_s.at[far, half], half_z.at[k], 30, device(x, y, z + 2 * s, core))
        send(sib_s.at[(z + 3 * s + 8) % 8], full_z.at[k], 23, device(x, y, z + s, core))
        send(sib_s.at[(z + s + 8) % 8], get_t.at[k], 31, device(x, y, z + s, core))
    due[23] = sent[23] = full_z
    due[30] = sent[30] = half_z

    arrive(3)
    send(feat_t.at[core], feat_t.at[core], 20, sibling)
    due[20] = sent[20] = feat_t.at[0]
    arrive(2)
    feat_it[...] = feat_i[...].reshape(256, 1280).T
    arrive(20)
    feat_tt[...] = feat_t[...].reshape(256, 1280).T

    arrive(29)
    for k in range(1, 4):
        px = (x + k) % 4
        total = own_i[y, px, 1]
        for j in range(1, 4):
            total += get_y[(y + j) % 4, px].astype(F32)
        dem_y2[px] = total.astype(BF16)
        send(dem_y2.at[px], last_y.at[x], 32, device(px, y, z, core))
    due[32] = sent[32] = last_y.at[pl.ds(0, 3)]
    arrive(22)
    for k in range(1, 4):
        py = (y + k) % 4
        total = own_i[py, x, 0]
        for j in range(1, 4):
            total += get_x[(x + j) % 4, py].astype(F32)
        dem_x2[py] = total.astype(BF16)
        send(dem_x2.at[py], last_x.at[y], 33, device(x, py, z, core))
    due[33] = sent[33] = last_x.at[pl.ds(0, 3)]
    arrive(23)
    arrive(30)
    for k, s in enumerate((1, -1)):
        dest = (z + 2 * s + 8) % 8
        total = own_t[dest] + full_z[k].astype(F32)
        extra = half_z[k].astype(F32)
        blank = jnp.zeros_like(extra)
        total += jnp.concatenate([extra, blank] if k == 0 else [blank, extra], axis=0)
        sum_z[k] = total.astype(BF16)
        send(sum_z.at[k], get_t.at[2 + k], 31, device(x, y, z + 2 * s, core))
    due[31] = sent[31] = get_t

    def split(total, invs, upper):
        draw = jnp.where(upper, invs[:, 256:512], invs[:, 0:256]) * total
        high = draw.astype(BF16)
        return high, (draw - high.astype(F32)).astype(BF16)

    def weights(f, draw):
        high, low = draw
        out = lax.dot_general(f, high, NT, preferred_element_type=F32)
        out += lax.dot_general(f, low, NT, preferred_element_type=F32)
        return out.reshape(-1, 80, 128)

    def image_sum(own, first, lines, last, at):
        total = own
        for j in range(1, 4):
            total += first((at + j) % 4).astype(F32)
            total += last[(lines + j) % 4].astype(F32)
        return total

    arrive(32)
    arrive(33)
    upper_cols = image_sum(own_i[y, x, 0], lambda j: get_x[j, y], y, last_x, x)
    lower_cols = image_sum(own_i[y, x, 1], lambda j: get_y[j, x], x, last_y, y)
    total_i = jnp.concatenate([upper_cols, lower_cols], axis=0)
    draw_i = split(total_i, invs_i, y % 2 == 1)

    def image_rows(k, owner):
        return weights(feat_it[pl.ds(pl.multiple_of(640 * k + 320 * owner, 320), 320), :], draw_i)

    for k in range(2):
        out_s[k] = image_rows(k, 1 - core)
    send(out_s, out_r, 25, sibling)
    due[25] = sent[25] = out_r
    for k in range(2):
        par_i[k] = image_rows(k, core)

    arrive(31)
    total_t = own_t[z] + jnp.sum(get_t[...].astype(F32), axis=0)
    par_t[...] = weights(feat_tt[...], split(total_t, invs_t, z // 4 == 1)).astype(BF16)

    def part_t(k):
        px, py = (x + k % 4) % 4, (y + k // 4) % 4
        send(par_t.at[px * 4 + text_pair(py)], sum_t.at[slot_i], 24, plane_peer(k))

    each(PLANE, part_t)
    due[24] = sent[24] = sum_t.at[pl.ds(0, 15)]
    sum_t[slot_i] = par_t[x * 4 + text_pair(y)]

    arrive(25)
    line_s[...] = (par_i[...] + out_r[...]).astype(BF16)

    def part_i(k):
        pz = (z + k) % 8
        send(line_s.at[pz % 2, pz // 2], sum_i.at[z], 26, line_peer(k))

    each(COLUMN, part_i)
    due[26] = sent[26] = sum_i.at[pl.ds(0, 7)]
    sum_i[z] = line_s[z % 2, z // 2]

    def last(total, fin, flag, slot, to, sem):
        for k in range(4):
            fin[0, k, 0:20, :] = total[20 * k:20 * k + 20, :]
            if flag is None:
                send(fin.at[0, k], fin.at[1, slot], sem, to(k))
                continue

            @pl.when(jnp.logical_not(flag & (k == quarter)))
            def _():
                send(fin.at[0, k], fin.at[1, slot], sem, to(k))

        if flag is not None:
            @pl.when(flag)
            def _():
                fin[1, slot] = fin[0, quarter]

    def wait_last(fin, flag, sem):
        if flag is None:
            drain(fin.at[0], sem)
            return

        @pl.when(flag)
        def _():
            drain(fin.at[0, pl.ds(0, 3)], sem)

        @pl.when(jnp.logical_not(flag))
        def _():
            drain(fin.at[0], sem)

    arrive(24)
    last(jnp.sum(sum_t[...].astype(F32), axis=0), fin_t, None, (z // 4) * 2 + z % 2, to_t, 27)
    arrive(26)
    last(jnp.sum(sum_i[...].astype(F32), axis=0), fin_i, self_i, (y % 2) * 2 + x % 2, to_i, 28)

    def finish(o_ref, fin, flag, sem):
        wait_last(fin, flag, rsem.at[sem])
        for k in range(2):
            o_ref[:, 128 * k:128 * k + 128] = fin[1, k, 0:20, :] + fin[1, 2 + k, 0:20, :]

    finish(o_ref.at[0], fin_i, self_i, 28)
    finish(o_ref.at[1], fin_t, None, 27)

    for i, ref in sent.items():
        drain(ref, ssem.at[i])
    wait_last(fin_t, None, ssem.at[27])
    wait_last(fin_i, self_i, ssem.at[28])


def per_device(feat_img, feat_txt, w_img, w_txt, logit_scale):
    v = pl.BlockSpec(memory_space=pltpu.VMEM)
    out = jax.ShapeDtypeStruct((2, 20, 256), F32)
    vm = pltpu.VMEM
    o = pl.pallas_call(
        kernel,
        out_shape=out,
        in_specs=[pl.BlockSpec(memory_space=pltpu.SMEM)] + [pl.BlockSpec(memory_space=pl.ANY)] * 4,
        out_specs=v,
        scratch_shapes=[
            vm((2, 2, 32, 1280), BF16), vm((2, 2, 32, 1280), BF16), vm((1280, 256), BF16), vm((1280, 256), BF16),
            vm((2, 4, 32, 256), F32), vm((2, 4, 32, 256), F32),
            vm((512, 1024), BF16), vm((512, 1024), BF16),
            vm((4, 2, 32, 1280), BF16), vm((2, 4, 32, 1280), BF16),
            vm((1024, 512), BF16), vm((1024, 512), BF16),
            vm((1280, 256), BF16), vm((1280, 256), BF16),
            vm((16, 8, 128), F32), vm((16, 8, 128), F32),
            vm((512, 512), F32), vm((512, 512), F32),
            vm((4, 4, 2, 64, 256), F32),
            vm((4, 4, 64, 256), BF16), vm((4, 4, 64, 256), BF16), vm((4, 4, 64, 256), BF16), vm((4, 4, 64, 256), BF16),
            vm((4, 64, 256), BF16), vm((4, 64, 256), BF16), vm((4, 64, 256), BF16), vm((4, 64, 256), BF16),
            vm((8, 128, 256), F32), vm((2, 4, 128, 256), BF16), vm((2, 4, 128, 256), BF16),
            vm((8, 128, 256), BF16), vm((2, 128, 256), BF16), vm((2, 64, 256), BF16), vm((2, 128, 256), BF16),
            vm((4, 128, 256), BF16),
            vm((2, 4, 80, 128), F32), vm((16, 80, 128), BF16), vm((2, 4, 80, 128), BF16),
            vm((8, 80, 128), BF16), vm((16, 80, 128), BF16),
            vm((2, 4, 80, 128), F32), vm((2, 4, 80, 128), F32),
            vm((2, 4, 24, 128), F32), vm((2, 4, 24, 128), F32),
            pltpu.SemaphoreType.DMA((34,)), pltpu.SemaphoreType.DMA((34,)), pltpu.SemaphoreType.DMA((4,)),
        ],
        compiler_params=pltpu.CompilerParams(
            collective_id=0, has_side_effects=True, vmem_limit_bytes=56 * 2 ** 20),
        name="contrastive",
    )(logit_scale.reshape(1, 1), feat_img.reshape(2, 2, 32, 1280), feat_txt.reshape(2, 2, 32, 1280), w_img, w_txt)
    return o[0], o[1]


def solution(mesh):
    return jax.shard_map(
        per_device,
        mesh=mesh,
        in_specs=(P("dp", None), P("dp", None), P(None, "head"), P(None, "head"), P()),
        out_specs=(P("dp", "head"), P("dp", "head")),
        check_vma=False,
    )
```

```python
import jax
import jax.numpy as jnp
from jax import lax
from jax.experimental import pallas as pl
from jax.experimental.pallas import tpu as pltpu
from jax.sharding import PartitionSpec as P

MESH = pl.DeviceIdType.MESH
F32 = jnp.float32
BF16 = jnp.bfloat16
NT = (((1,), (1,)), ((), ()))
NN = (((1,), (0,)), ((), ()))


def device(x, y, z, core):
    x, y, z = (x + 4) % 4, (y + 4) % 4, (z + 8) % 8
    return {"dp": (x * 8 + z) * 2 + y % 2, "head": (y // 2) * 2 + core}


def place():
    d = lax.axis_index("dp")
    h = lax.axis_index("head")
    return d // 16, (h // 2) * 2 + d % 2, (d // 2) % 8, h % 2


def image_slot(x, y):
    x, y = (x + 4) % 4, (y + 4) % 4
    return (y % 2) * 8 + x * 2 + y // 2


def text_slot(z, core):
    z = (z + 8) % 8
    return (z // 4) * 8 + core * 4 + z % 4


def rows(slot, count=32, shift=0):
    return pl.ds(pl.multiple_of(slot * 32 + shift, 16), count)


def drain(ref, sem):
    pltpu.make_async_copy(ref, ref, sem).wait()


def each(steps, body):
    for k in steps:
        body(k)


def hops(k, n):
    return min(k % n, n - k % n)


PLANE = sorted(range(1, 16), key=lambda k: -hops(k, 4) - hops(k // 4, 4))
LINE = sorted(range(1, 16), key=lambda k: -hops(k, 8))
COLUMN = [k for k in LINE if k < 8]


def to_column(row):
    eye = lax.broadcasted_iota(jnp.int32, (128, 128), 0) == lax.broadcasted_iota(jnp.int32, (128, 128), 1)
    return jnp.concatenate(
        [jnp.sum(jnp.where(eye, row[:, 128 * k:128 * k + 128], 0.0), axis=1, keepdims=True)
         for k in range(row.shape[1] // 128)], axis=0)


def lse_rows(a):
    top = jnp.max(a, axis=0, keepdims=True)
    return top + jnp.log(jnp.sum(jnp.exp(a - top), axis=0, keepdims=True))


def put_stats(ref, lse, inv):
    for k in range(4):
        ref[k:k + 1, :] = lse[:, 128 * k:128 * k + 128]
    pick = lax.broadcasted_iota(jnp.int32, (32, 128), 0) == lax.broadcasted_iota(jnp.int32, (32, 128), 1)
    ref[4:5, :] = jnp.sum(jnp.where(pick, inv, 0.0), axis=0, keepdims=True)


def merged_stats(ref):
    a = ref[:, 0:4, :]
    top = jnp.max(a, axis=0)
    lse = top + jnp.log(jnp.sum(jnp.exp(a - top[None]), axis=0))
    lse = jnp.concatenate([lse[k:k + 1, :] for k in range(4)], axis=1)
    inv = jnp.concatenate([ref[k, 4:5, 0:32] for k in range(16)], axis=1)
    return lse, inv


def kernel(scale_ref, fi_ref, ft_ref, wi_ref, wt_ref, o_ref,
           fi_v, ft_v, wi_v, wt_v,
           raw_s, raw_r, emb_i, emb_t, feat_i, feat_t, emb_it, emb_tt, feat_it, feat_tt,
           stat_i, stat_t, log_a, log_b, own_i, dem_x, dem_y, get_x, get_y, dem_x2, dem_y2, last_x, last_y,
           own_t, dem_t, sib_r, sib_s, full_z, half_z, sum_z, get_t,
           par_i, par_t, line_s, sum_i, sum_t, out_s, out_r, fin_i, fin_t, ssem, rsem, lsem):
    x, y, z, core = place()
    h = lax.axis_index("head")
    slot_i = image_slot(x, y)
    slot_t = text_slot(z, core)
    sibling = device(x, y, z, 1 - core)
    due = {}
    sent = {}

    def send(src, dst, sem, peer, arrival=None):
        pltpu.make_async_remote_copy(
            src_ref=src, dst_ref=dst, send_sem=ssem.at[sem], recv_sem=rsem.at[sem if arrival is None else arrival],
            device_id=peer, device_id_type=MESH,
        ).start()

    def arrive(i):
        drain(due.pop(i), rsem.at[i])

    def head_peer(k):
        return {"dp": lax.axis_index("dp"), "head": (h + k) % 4}

    def plane_peer(k):
        return device(x + k % 4, y + k // 4, z, core)

    def line_peer(k):
        return device(x, y, z + k % 8, (core + k // 8) % 2)

    self_i = (z % 2 == x // 2) & (core == x % 2) & (core == x // 2)
    quarter = (z % 2) * 2 + y % 2

    def to_i(e):
        return device((z % 2) * 2 + core, (y // 2) * 2 + e % 2, (z // 2) * 2 + e // 2, x // 2)

    def text_pair(py):
        step = 1 - 2 * (z % 2)
        inside = jnp.where(py % 2 == 0, 2, step)
        outside = jnp.where(py % 2 == 0, -step, 0)
        return (z // 2 + jnp.where(py // 2 == core, inside, outside) + 4) % 4

    def to_t(e):
        return device(x, core * 2 + e % 2, 2 * text_pair(y) + e // 2, (z % 4) // 2)

    bar = pltpu.get_barrier_semaphore()

    def hello(peer):
        pl.semaphore_signal(bar, inc=1, device_id=peer, device_id_type=MESH)

    each(range(1, 4), lambda k: hello(head_peer(k)))
    each(range(1, 4), lambda k: hello(device(x + k, y, z, core)))
    hello(device(x, y + 1, z, core))
    hello(device(x, y - 1, z, core))
    each(range(1, 4), lambda k: hello(device(x, y, z + k, core)))
    each(range(1, 4), lambda k: hello(device(x, y, z - k, core)))

    fetched = [pltpu.make_async_copy(a, b, lsem.at[k])
               for k, (a, b) in enumerate(((fi_ref, fi_v), (wi_ref, wi_v), (ft_ref, ft_v), (wt_ref, wt_v)))]
    for copy in fetched:
        copy.start()

    for side, (f, w) in enumerate(((fi_v, wi_v), (ft_v, wt_v))):
        fetched[2 * side].wait()
        fetched[2 * side + 1].wait()
        raw = jnp.dot(f[...].reshape(128, 1280), w[...], preferred_element_type=F32)
        raw_s[side] = raw.reshape(4, 32, 256)

    pl.semaphore_wait(bar, 14)

    def send_raw(side, sem):
        def one(k):
            peer = head_peer(k)
            send(raw_s.at[side, peer["head"]], raw_r.at[side, h], sem, peer)
        each(range(1, 4), one)
        due[sem] = sent[sem] = raw_s.at[side, pl.ds(0, 3)]
        raw_r[side, h] = raw_s[side, h]

    send_raw(0, 0)
    send_raw(1, 1)

    def unit_rows(side):
        whole = jnp.concatenate([raw_r[side, k] for k in range(4)], axis=1)
        inv = lax.rsqrt(jnp.sum(whole * whole, axis=1, keepdims=True) + 1e-06)
        return (whole * inv).astype(BF16), inv

    order = (1, 3, 2)
    mine_i = rows(slot_i)
    mine_t = rows(slot_t)
    arrive(0)
    unit_i, inv_i = unit_rows(0)
    emb_i[mine_i, :] = unit_i
    for k in order:
        send(emb_i.at[mine_i], emb_i.at[mine_i], 4, device(x + k, y, z, core), 4 + k)
        send(emb_i.at[mine_i], emb_i.at[mine_i], 4, device(x, y + k, z, core), 7 + k)
        due[4 + k] = due[7 + k] = emb_i.at[rows(0)]
    arrive(1)
    unit_t, inv_t = unit_rows(1)
    emb_t[mine_t, :] = unit_t
    for k, s in enumerate((2, -2, 1, -1)):
        send(emb_t.at[mine_t], emb_t.at[mine_t], 12, device(x, y, z + s, core), 12 + k)
        due[12 + k] = emb_t.at[rows(0)]

    def forward_x(k):
        arrive(4 + k)
        block = rows(image_slot(x - k, y), 16)
        for j in order:
            send(emb_i.at[block], emb_i.at[block], 4, device(x, y + j, z, core), 11)

    def forward_y(k):
        arrive(7 + k)
        block = rows(image_slot(x, y - k), 16, 16)
        for j in order:
            send(emb_i.at[block], emb_i.at[block], 4, device(x + j, y, z, core), 11)

    def forward_z(k, s):
        arrive(12 + k)
        block = rows(text_slot(z + 2 * s, core))
        send(emb_t.at[block], emb_t.at[block], 12, device(x, y, z - s, core), 16)
        block = rows(text_slot(z + 2 * s, core), 16, 16 * k)
        send(emb_t.at[block], emb_t.at[block], 12, device(x, y, z - 2 * s, core), 16)

    def to_sibling(z_from):
        block = rows(text_slot(z_from, core))
        send(emb_t.at[block], emb_t.at[block], 17, sibling)

    to_sibling(z)
    forward_x(1)
    forward_y(1)
    forward_x(3)
    forward_y(3)
    forward_z(0, -1)
    forward_z(1, 1)
    forward_x(2)
    forward_y(2)
    due[11] = emb_i.at[rows(0, 288)]
    due[16] = emb_t.at[rows(0, 96)]
    sent[4] = emb_i.at[rows(0, 480)]
    sent[12] = emb_t.at[rows(0, 224)]
    to_sibling(z - 2)
    to_sibling(z + 2)
    arrive(14)
    to_sibling(z - 1)
    arrive(15)
    to_sibling(z + 1)
    arrive(16)
    to_sibling(z + 3)
    to_sibling(z - 3)
    to_sibling(z + 4)
    due[17] = sent[17] = emb_t.at[pl.ds(0, 256)]
    arrive(11)

    scale = scale_ref[0, 0]

    def logits(part):
        where = [pl.ds(pl.multiple_of(256 * k + 128 * part, 128), 128) for k in range(2)]
        texts = jnp.concatenate([emb_t[r, :] for r in where], axis=0)
        a = scale * lax.dot_general(texts, emb_i[...], NT, preferred_element_type=F32)
        for k in range(2):
            log_b[where[k], :] = a[128 * k:128 * k + 128]

    logits(core)
    arrive(17)
    logits(1 - core)
    put_stats(stat_i.at[slot_i], lse_rows(log_b[...]), inv_i)
    each(PLANE, lambda k: send(stat_i.at[slot_i], stat_i.at[slot_i], 18, plane_peer(k)))
    due[18] = sent[18] = stat_i.at[pl.ds(0, 15)]
    log_a[...] = log_b[...].T
    put_stats(stat_t.at[slot_t], lse_rows(log_a[...]), inv_t)
    each(LINE, lambda k: send(stat_t.at[slot_t], stat_t.at[slot_t], 19, line_peer(k)))
    due[19] = sent[19] = stat_t.at[pl.ds(0, 15)]
    each(range(1, 4), lambda k: send(fi_v.at[:, core], feat_i.at[x], 2, device(x + k, y, z, core)))
    due[2] = sent[2] = feat_i.at[pl.ds(0, 3)]
    feat_i[x] = fi_v[:, core]
    each(range(1, 4), lambda k: send(ft_v.at[y // 2, core], feat_t.at[core, z % 4], 3,
                              device(x, y, (z // 4) * 4 + (z + k) % 4, core)))
    due[3] = sent[3] = feat_t.at[0, pl.ds(0, 3)]
    feat_t[core, z % 4] = ft_v[y // 2, core]

    emb_it[...] = emb_i[...].T
    emb_tt[...] = emb_t[...].T
    arrive(18)
    arrive(19)
    row_lse, invs_i = merged_stats(stat_i)
    col_lse, invs_t = merged_stats(stat_t)

    factor = 1.0 / (2.0 * (64.0 * 2.0 ** 0.5))
    ids0 = lax.broadcasted_iota(jnp.int32, (512, 512), 0)
    ids1 = lax.broadcasted_iota(jnp.int32, (512, 512), 1)

    a = log_a[...]
    same = (ids0 // 32 == slot_i) & (ids0 - ids1 == 32 * (slot_i - slot_t))
    g = (jnp.exp(a - to_column(row_lse)) + jnp.exp(a - col_lse) - jnp.where(same, 2.0, 0.0)) * factor
    g = g.astype(BF16)
    inner_t = jnp.sum(g.astype(F32) * a, axis=0, keepdims=True)

    def demb(g, inner, base, unit, half):
        part = pl.ds(pl.multiple_of(512 * half, 512), 512)
        d = scale * lax.dot_general(base[part, :], g, NN, preferred_element_type=F32)
        return d - unit[part, :].astype(F32) * inner

    d = demb(g, inner_t, emb_it, emb_tt, 1 - core)
    for k in range(2):
        dem_t[k] = d[:, 256 * k:256 * k + 256].astype(BF16).reshape(4, 128, 256)
        send(dem_t.at[k], sib_r.at[k], 21, sibling)
    due[21] = sent[21] = sib_r
    gt = g.T
    inner_i = jnp.sum(gt.astype(F32) * log_b[...], axis=0, keepdims=True)

    def image_half(pair):
        d = demb(gt, inner_i, emb_tt, emb_it, pair)
        for k in range(2):
            py = 2 * pair + k
            e = d[:, 256 * k:256 * k + 256].reshape(4, 2, 64, 256)
            own_i[py] = e
            dem_x[:, py] = e[:, 0].astype(BF16)
            dem_y[py] = e[:, 1].astype(BF16)

    def send_y(py):
        send(dem_y.at[py], get_y.at[y], 29, device(x, py, z, core))

    image_half(1 - y // 2)
    send_y((y + 2) % 4)
    send_y((1 - y // 2) * 2 + (y + 1) % 2)
    image_half(y // 2)
    each(range(0, 3), lambda k: send(dem_x.at[(x + 1 + (k + 1) % 3) % 4], get_x.at[x], 22, device(x + 1 + (k + 1) % 3, y, z, core)))
    send_y((y // 2) * 2 + (y + 1) % 2)
    due[22] = sent[22] = get_x.at[pl.ds(0, 3)]
    due[29] = sent[29] = get_y.at[pl.ds(0, 3)]
    d = demb(g, inner_t, emb_it, emb_tt, core)
    for k in range(2):
        own_t[4 * k:4 * k + 4] = d[:, 256 * k:256 * k + 256].reshape(4, 128, 256)

    arrive(21)
    own_t[...] = own_t[...] + sib_r[...].astype(F32).reshape(8, 128, 256)
    sib_s[...] = own_t[...].astype(BF16)
    for k, s in enumerate((1, -1)):
        far = (z + 4) % 8
        half = pl.ds(64 * k, 64)
        send(sib_s.at[far, half], half_z.at[k], 30, device(x, y, z + 2 * s, core))
        send(sib_s.at[(z + 3 * s + 8) % 8], full_z.at[k], 23, device(x, y, z + s, core))
        send(sib_s.at[(z + s + 8) % 8], get_t.at[k], 31, device(x, y, z + s, core))
    due[23] = sent[23] = full_z
    due[30] = sent[30] = half_z

    arrive(3)
    send(feat_t.at[core], feat_t.at[core], 20, sibling)
    due[20] = sent[20] = feat_t.at[0]
    arrive(2)
    feat_it[...] = feat_i[...].reshape(256, 1280).T
    arrive(20)
    feat_tt[...] = feat_t[...].reshape(256, 1280).T

    arrive(29)
    for k in range(1, 4):
        px = (x + k) % 4
        total = own_i[y, px, 1]
        for j in range(1, 4):
            total += get_y[(y + j) % 4, px].astype(F32)
        dem_y2[px] = total.astype(BF16)
        send(dem_y2.at[px], last_y.at[x], 32, device(px, y, z, core))
    due[32] = sent[32] = last_y.at[pl.ds(0, 3)]
    arrive(22)
    for k in range(1, 4):
        py = (y + k) % 4
        total = own_i[py, x, 0]
        for j in range(1, 4):
            total += get_x[(x + j) % 4, py].astype(F32)
        dem_x2[py] = total.astype(BF16)
        send(dem_x2.at[py], last_x.at[y], 33, device(x, py, z, core))
    due[33] = sent[33] = last_x.at[pl.ds(0, 3)]
    arrive(23)
    arrive(30)
    for k, s in enumerate((1, -1)):
        dest = (z + 2 * s + 8) % 8
        total = own_t[dest] + full_z[k].astype(F32)
        extra = half_z[k].astype(F32)
        blank = jnp.zeros_like(extra)
        total += jnp.concatenate([extra, blank] if k == 0 else [blank, extra], axis=0)
        sum_z[k] = total.astype(BF16)
        send(sum_z.at[k], get_t.at[2 + k], 31, device(x, y, z + 2 * s, core))
    due[31] = sent[31] = get_t

    def split(total, invs, upper):
        draw = jnp.where(upper, invs[:, 256:512], invs[:, 0:256]) * total
        high = draw.astype(BF16)
        return high, (draw - high.astype(F32)).astype(BF16)

    def weights(f, draw):
        high, low = draw
        out = lax.dot_general(f, high, NT, preferred_element_type=F32)
        out += lax.dot_general(f, low, NT, preferred_element_type=F32)
        return out.reshape(-1, 80, 128)

    def image_sum(own, first, lines, last, at):
        total = own
        for j in range(1, 4):
            total += first((at + j) % 4).astype(F32)
            total += last[(lines + j) % 4].astype(F32)
        return total

    arrive(32)
    arrive(33)
    upper_cols = image_sum(own_i[y, x, 0], lambda j: get_x[j, y], y, last_x, x)
    lower_cols = image_sum(own_i[y, x, 1], lambda j: get_y[j, x], x, last_y, y)
    total_i = jnp.concatenate([upper_cols, lower_cols], axis=0)
    draw_i = split(total_i, invs_i, y % 2 == 1)

    def image_rows(k, owner):
        return weights(feat_it[pl.ds(pl.multiple_of(640 * k + 320 * owner, 320), 320), :], draw_i)

    for k in range(2):
        out_s[k] = image_rows(k, 1 - core)
        send(out_s.at[k], out_r.at[k], 25, sibling)
    due[25] = sent[25] = out_r
    for k in range(2):
        par_i[k] = image_rows(k, core)

    arrive(31)
    total_t = own_t[z] + jnp.sum(get_t[...].astype(F32), axis=0)
    par_t[...] = weights(feat_tt[...], split(total_t, invs_t, z // 4 == 1)).astype(BF16)

    def part_t(k):
        px, py = (x + k % 4) % 4, (y + k // 4) % 4
        send(par_t.at[px * 4 + text_pair(py)], sum_t.at[slot_i], 24, plane_peer(k))

    each(PLANE, part_t)
    due[24] = sent[24] = sum_t.at[pl.ds(0, 15)]
    sum_t[slot_i] = par_t[x * 4 + text_pair(y)]

    arrive(25)
    line_s[...] = (par_i[...] + out_r[...]).astype(BF16)

    def part_i(k):
        pz = (z + k) % 8
        send(line_s.at[pz % 2, pz // 2], sum_i.at[z], 26, line_peer(k))

    each(COLUMN, part_i)
    due[26] = sent[26] = sum_i.at[pl.ds(0, 7)]
    sum_i[z] = line_s[z % 2, z // 2]

    def last(total, fin, flag, slot, to, sem):
        for k in range(4):
            fin[0, k, 0:20, :] = total[20 * k:20 * k + 20, :]
            if flag is None:
                send(fin.at[0, k], fin.at[1, slot], sem, to(k))
                continue

            @pl.when(jnp.logical_not(flag & (k == quarter)))
            def _():
                send(fin.at[0, k], fin.at[1, slot], sem, to(k))

        if flag is not None:
            @pl.when(flag)
            def _():
                fin[1, slot] = fin[0, quarter]

    def wait_last(fin, flag, sem):
        if flag is None:
            drain(fin.at[0], sem)
            return

        @pl.when(flag)
        def _():
            drain(fin.at[0, pl.ds(0, 3)], sem)

        @pl.when(jnp.logical_not(flag))
        def _():
            drain(fin.at[0], sem)

    arrive(24)
    last(jnp.sum(sum_t[...].astype(F32), axis=0), fin_t, None, (z // 4) * 2 + z % 2, to_t, 27)
    arrive(26)
    last(jnp.sum(sum_i[...].astype(F32), axis=0), fin_i, self_i, (y % 2) * 2 + x % 2, to_i, 28)

    def finish(o_ref, fin, flag, sem):
        wait_last(fin, flag, rsem.at[sem])
        for k in range(2):
            o_ref[:, 128 * k:128 * k + 128] = fin[1, k, 0:20, :] + fin[1, 2 + k, 0:20, :]

    finish(o_ref.at[0], fin_i, self_i, 28)
    finish(o_ref.at[1], fin_t, None, 27)

    for i, ref in sent.items():
        drain(ref, ssem.at[i])
    wait_last(fin_t, None, ssem.at[27])
    wait_last(fin_i, self_i, ssem.at[28])


def per_device(feat_img, feat_txt, w_img, w_txt, logit_scale):
    v = pl.BlockSpec(memory_space=pltpu.VMEM)
    out = jax.ShapeDtypeStruct((2, 20, 256), F32)
    vm = pltpu.VMEM
    o = pl.pallas_call(
        kernel,
        out_shape=out,
        in_specs=[pl.BlockSpec(memory_space=pltpu.SMEM)] + [pl.BlockSpec(memory_space=pl.ANY)] * 4,
        out_specs=v,
        scratch_shapes=[
            vm((2, 2, 32, 1280), BF16), vm((2, 2, 32, 1280), BF16), vm((1280, 256), BF16), vm((1280, 256), BF16),
            vm((2, 4, 32, 256), F32), vm((2, 4, 32, 256), F32),
            vm((512, 1024), BF16), vm((512, 1024), BF16),
            vm((4, 2, 32, 1280), BF16), vm((2, 4, 32, 1280), BF16),
            vm((1024, 512), BF16), vm((1024, 512), BF16),
            vm((1280, 256), BF16), vm((1280, 256), BF16),
            vm((16, 8, 128), F32), vm((16, 8, 128), F32),
            vm((512, 512), F32), vm((512, 512), F32),
            vm((4, 4, 2, 64, 256), F32),
            vm((4, 4, 64, 256), BF16), vm((4, 4, 64, 256), BF16), vm((4, 4, 64, 256), BF16), vm((4, 4, 64, 256), BF16),
            vm((4, 64, 256), BF16), vm((4, 64, 256), BF16), vm((4, 64, 256), BF16), vm((4, 64, 256), BF16),
            vm((8, 128, 256), F32), vm((2, 4, 128, 256), BF16), vm((2, 4, 128, 256), BF16),
            vm((8, 128, 256), BF16), vm((2, 128, 256), BF16), vm((2, 64, 256), BF16), vm((2, 128, 256), BF16),
            vm((4, 128, 256), BF16),
            vm((2, 4, 80, 128), F32), vm((16, 80, 128), BF16), vm((2, 4, 80, 128), BF16),
            vm((8, 80, 128), BF16), vm((16, 80, 128), BF16),
            vm((2, 4, 80, 128), F32), vm((2, 4, 80, 128), F32),
            vm((2, 4, 24, 128), F32), vm((2, 4, 24, 128), F32),
            pltpu.SemaphoreType.DMA((34,)), pltpu.SemaphoreType.DMA((34,)), pltpu.SemaphoreType.DMA((4,)),
        ],
        compiler_params=pltpu.CompilerParams(
            collective_id=0, has_side_effects=True, vmem_limit_bytes=56 * 2 ** 20),
        name="contrastive",
    )(logit_scale.reshape(1, 1), feat_img.reshape(2, 2, 32, 1280), feat_txt.reshape(2, 2, 32, 1280), w_img, w_txt)
    return o[0], o[1]


def solution(mesh):
    return jax.shard_map(
        per_device,
        mesh=mesh,
        in_specs=(P("dp", None), P("dp", None), P(None, "head"), P(None, "head"), P()),
        out_specs=(P("dp", "head"), P("dp", "head")),
        check_vma=False,
    )
```
